512 devices in a mesh: row: 16 (over z), col: 32 (over x, y, core).
Axes of the slice: x: 4, y: 4, z: 16, core: 2. Of those that a mesh axis runs over, the one named last changes fastest.
Arguments:
- jacobians: bfloat16 [1024, 60, 190], P(('row', 'col')), may hold values from -0.4375 to 0.4375
- descriptors: bfloat16 [1024, 190], P(('row', 'col')), may hold values from -6 to 6
- block_inverse: bfloat16 [960, 960], replicated
- tile_order: int32 [1024], replicated, may hold values from 0 to 1023, each once
- panel: int32 [1], replicated, may hold values from 0 to 62
Outputs:
- panel_factor: bfloat16 [61440, 960], P(('row', 'col'))
- next_column: bfloat16 [61440, 960], P(('row', 'col'))
The draws below stay inside these ranges and needn't reach their ends.
Inputs may be any that keep to these rules, and one draw needn't show every extreme that they name: `tile_order`: each conformer once. The next panel exists.
All inputs are finite; a program needn't handle non-finite values.
Results may differ from the reference program's by a relative error of at most 0.0051.
Values may be sent and summed in bfloat16 or wider, within the bound.
A program may use at most 64 MiB of HBM per device.

```python
import math
import jax
import jax.numpy as jnp
from jax import lax

NCOMP = 60
NDESC = 190
PC = 16
ROWS_DEV = 2
CONF = 1024
PCOLS = 960


def draw_block_inverse(key, part):
    key = jax.random.fold_in(key, 7)
    key_diag, key_off = jax.random.split(key)
    diag = jnp.exp(jax.random.uniform(key_diag, (PCOLS,), jnp.float32, -0.7, 0.7))
    off = jax.random.normal(key_off, (PCOLS, PCOLS), jnp.float32)
    off = off * jnp.float32(PCOLS) ** (-0.5)
    index = jnp.arange(PCOLS)
    lower = index[:, None] > index[None, :]
    matrix = jnp.where(lower, off, 0.0) + jnp.where(index[:, None] == index[None, :], diag[:, None], 0.0)
    return matrix.astype(jnp.bfloat16)


def shard_levels(stream_key, shape, shards, smallest, largest):
    def one(position, blocks):
        heights = jax.random.uniform(jax.random.fold_in(jax.random.fold_in(stream_key, 6), position), (blocks,), jnp.float32, smallest / len(shards), largest / len(shards))
        return jnp.repeat(jnp.exp(heights), shape[position] // blocks).reshape((-1,) + (1,) * (len(shape) - position - 1))

    gain = one(*shards[0])
    for cut in shards[1:]:
        gain = gain * one(*cut)
    return gain


def scatter_about(own_key, dims, spread, most, pieces=(), dtype=jnp.bfloat16):
    entries = jax.random.normal(own_key, dims, jnp.float32) * spread
    if len(pieces) > 0:
        entries = shard_levels(own_key, dims, pieces, -0.22, 0.18) * entries
    return jnp.clip(entries, min=-most, max=most).astype(dtype)


def setup_inputs(seed: int = 0) -> dict:
    splits = jax.random.split(jax.random.key(seed), 6)
    jacobians = scatter_about(splits[0], (CONF, NCOMP, NDESC), NDESC ** -0.5, 0.4375, ((0, 512),))
    descriptors = scatter_about(splits[1], (CONF, NDESC), 1.0, 6.0, ((0, 512),))
    block_inverse = draw_block_inverse(jax.random.fold_in(splits[5], 71), 0)
    tile_order = jax.random.permutation(splits[3], CONF).astype(jnp.int32)
    panel = jax.random.randint(splits[4], (1,), 0, CONF // PC - 1).astype(jnp.int32)
    return dict(jacobians=jacobians, descriptors=descriptors, block_inverse=block_inverse, tile_order=tile_order, panel=panel)


def kernel_block(jac_rows, desc_rows, jac_cols, desc_cols):
    count_a, ncomp, ndesc = jac_rows.shape
    count_b = jac_cols.shape[0]
    width = 2.0 * math.sqrt(2.0 * ndesc)
    inner = jnp.dot(jac_rows.reshape(count_a * ncomp, ndesc), jac_cols.reshape(count_b * ncomp, ndesc).T, preferred_element_type=jnp.float32)
    inner = inner.reshape(count_a, ncomp, count_b, ncomp)
    diff = desc_rows.astype(jnp.float32)[:, None, :] - desc_cols.astype(jnp.float32)[None, :, :]
    dist = jnp.sqrt(lax.optimization_barrier(jnp.sum(diff * diff, axis=-1)))
    scaled = math.sqrt(5.0) * dist / width
    decay = jnp.exp(-scaled)
    left = jnp.einsum('abd,acd->abc', diff, jac_rows.astype(jnp.float32), precision=lax.Precision.HIGHEST)
    right = jnp.einsum('abd,bed->abe', diff, jac_cols.astype(jnp.float32), precision=lax.Precision.HIGHEST)
    outer = jnp.einsum('abc,abe->acbe', left, right, precision=lax.Precision.HIGHEST)
    first = (decay * (1.0 + scaled))[:, None, :, None]
    second = (decay * (5.0 / (width * width)))[:, None, :, None]
    kern = first * inner - second * outer
    return kern.reshape(count_a * ncomp, count_b * ncomp)

def reference(jacobians, descriptors, block_inverse, tile_order, panel):
    start = (panel[0] * PC).astype(jnp.int32)
    ids_panel = lax.dynamic_slice(tile_order, (start,), (PC,))
    ids_next = lax.dynamic_slice(tile_order, (start + PC,), (PC,))
    jac_panel = jacobians[ids_panel]
    desc_panel = descriptors[ids_panel]
    jac_next = jacobians[ids_next]
    desc_next = descriptors[ids_next]
    cross = kernel_block(jac_panel, desc_panel, jac_next, desc_next).astype(jnp.bfloat16)
    solved = jnp.dot(block_inverse, cross, preferred_element_type=jnp.float32).astype(jnp.bfloat16)
    blocks = CONF // ROWS_DEV
    jac_blocks = jacobians.reshape(blocks, ROWS_DEV, NCOMP, NDESC)
    desc_blocks = descriptors.reshape(blocks, ROWS_DEV, NDESC)

    def one_block(pair):
        jac_here, desc_here = pair
        tiles = kernel_block(jac_here, desc_here, jac_panel, desc_panel).astype(jnp.bfloat16)
        factor = jnp.dot(tiles, block_inverse.T, preferred_element_type=jnp.float32).astype(jnp.bfloat16)
        fresh = kernel_block(jac_here, desc_here, jac_next, desc_next)
        updated = (fresh - jnp.dot(factor, solved, preferred_element_type=jnp.float32)).astype(jnp.bfloat16)
        return (factor, updated)
    factors, updates = lax.map(one_block, (jac_blocks, desc_blocks))
    return (factors.reshape(CONF * NCOMP, PCOLS), updates.reshape(CONF * NCOMP, PCOLS))
```

```python
import functools
import math

import jax
import jax.numpy as jnp
from jax import lax
from jax.experimental import pallas as pl
from jax.experimental.pallas import tpu as pltpu
from jax.sharding import PartitionSpec as P

MESH = pl.DeviceIdType.MESH
F32 = jnp.float32
BF16 = jnp.bfloat16
NC = 60
ND = 190
PB = 64
TR = 16
TL = 128
NZ = 16
NCH = 16
SLOTS = 32
CHUNKS = 12

NT = (((1,), (1,)), ((), ()))
NN = (((1,), (0,)), ((), ()))


def dot(a, b, dims):
    return lax.dot_general(a, b, dims, preferred_element_type=F32)


def own_blocks(jac_ref, desc_ref, blk, send1):
    blk[...] = jnp.zeros_like(blk)
    for i in range(2):
        jac = jac_ref[i]
        desc = desc_ref[i : i + 1, :]
        jac32 = jac.astype(F32)
        desc32 = desc.astype(F32)
        col = jnp.sum(jac32 * desc32, axis=1, keepdims=True)
        high = col.astype(BF16).astype(F32)
        row = dot(jnp.broadcast_to(desc32, (8, ND)).astype(BF16), jac, NT)[0:1, :]
        row_high = row.astype(BF16).astype(F32)
        blk[i, 0:NC, 0:ND] = jac32
        blk[i, 0:NC, ND : ND + 1] = high
        blk[i, 0:NC, ND + 1 : ND + 2] = col - high
        blk[i, NC : NC + 1, 0:ND] = desc32
        blk[i, NC + 1 : NC + 2, 0:NC] = row_high
        blk[i, NC + 1 : NC + 2, PB : PB + NC] = row_high
        blk[i, NC + 2 : NC + 3, 0:NC] = row - row_high
        blk[i, NC + 2 : NC + 3, PB : PB + NC] = row - row_high
    lane = lax.broadcasted_iota(jnp.int32, (TR, TL), 1)
    for r in range(4):
        rows = slice(TR * r, TR * r + TR)
        send1[2 * r] = blk[0, rows, 0:TL].astype(BF16)
        send1[2 * r + 1] = blk[1, rows, 0:TL].astype(BF16)
        first = blk[0, rows, TL : 2 * TL]
        second = pltpu.roll(blk[1, rows, TL : 2 * TL], 64, 1)
        send1[8 + r] = jnp.where(lane < 64, first, second).astype(BF16)


def exchange(
    order_ref, panel_ref, jac_ref, desc_ref, own_ref, all_ref,
    blk, got1, send2, got2, mine, s1, r1, s2, r2, s3, r3, s4, r4, s5, r5,
):
    z = lax.axis_index("row")
    col = lax.axis_index("col")
    core = col % 2
    chip = col // 2
    sib = chip * 2 + 1 - core

    barrier = pltpu.get_barrier_semaphore()
    for d in range(1, NZ):
        pl.semaphore_signal(barrier, inc=1, device_id=((z + d) % NZ, col), device_id_type=MESH)
    for d in range(1, 2 * NCH):
        pl.semaphore_signal(barrier, inc=1, device_id=(z, (col + d) % (2 * NCH)), device_id_type=MESH)
    own_blocks(jac_ref, desc_ref, blk, own_ref)
    pl.semaphore_wait(barrier, NZ - 1 + 2 * NCH - 1)

    holds = z < CHUNKS
    is_y = jnp.logical_and(z >= 4, z < 8)
    is_x = jnp.logical_and(holds, jnp.logical_or(z < 4, z >= 8))

    def part(k):
        return (2 * (k % 4), 2) if k < 4 or k >= 8 else (8 + k % 4, 1)

    for k in range(CHUNKS):
        first, n = part(k)

        def send(k=k, first=first, n=n):
            pltpu.make_async_remote_copy(
                own_ref.at[pl.ds(first, n)], got1.at[z, pl.ds(0, n)], s1, r1,
                device_id=(k, col), device_id_type=MESH,
            ).start()

        def keep(k=k, first=first, n=n):
            got1[k, 0:n] = own_ref[first : first + n]

        pl.when(z != k)(send)
        pl.when(z == k)(keep)

    def slot(s):
        conf = order_ref[panel_ref[0] * (SLOTS // 2) + s]
        return conf // (4 * NCH), (conf // 2) % (2 * NCH) == col, conf % 2

    zeros = jnp.zeros((TR, TL), F32)

    @pl.when(is_x)
    def _():
        pltpu.make_async_copy(got1.at[0 : NZ - 1], got1.at[0 : NZ - 1], r1).wait()

    @pl.when(is_y)
    def _():
        pltpu.make_async_copy(send2.at[0 : NZ - 1], send2.at[0 : NZ - 1], r1).wait()

    for odd in range(2):

        @pl.when(jnp.logical_and(is_x, (z >= 8) == (odd == 1)))
        def _(odd=odd):
            for j in range(NCH):
                where, hit, i = slot(2 * j + odd)
                tile = got1[where, i].astype(F32)
                send2[j] = jnp.where(hit, tile, zeros).astype(BF16)

    @pl.when(is_y)
    def _():
        lane = lax.broadcasted_iota(jnp.int32, (TR, TL), 1)
        for j in range(NCH):
            where0, hit0, i0 = slot(2 * j)
            where1, hit1, i1 = slot(2 * j + 1)
            t0 = got1[where0, 0].astype(F32)
            t1 = got1[where1, 0].astype(F32)
            t0 = jnp.where(i0 == 0, t0, pltpu.roll(t0, 64, 1))
            t1 = jnp.where(i1 == 1, t1, pltpu.roll(t1, 64, 1))
            t0 = jnp.where(hit0, t0, zeros)
            t1 = jnp.where(hit1, t1, zeros)
            send2[j] = jnp.where(lane < 64, t0, t1).astype(BF16)

    turn = z % 2

    @pl.when(holds)
    def _():
        for j in range(NCH):
            to = 2 * j + turn

            @pl.when(to != col)
            def _(j=j, to=to):
                pltpu.make_async_remote_copy(
                    send2.at[j], got2.at[(col + 2 * NCH - to) % (2 * NCH)], s2, r2,
                    device_id=(z, to), device_id_type=MESH,
                ).start()

            @pl.when(to == col)
            def _(j=j):
                got2[0] = send2[j]

    reduces = jnp.logical_and(holds, core == turn)
    place = z // 2

    @pl.when(reduces)
    def _():
        pltpu.make_async_copy(got2.at[1 : 2 * NCH], got2.at[1 : 2 * NCH], r2).wait()
        total = got2[0].astype(F32)
        for n in range(1, 2 * NCH):
            total = total + got2[n].astype(F32)
        mine[place] = total.astype(BF16)
        for d in range(1, NZ):
            pltpu.make_async_remote_copy(
                mine.at[place], mine.at[place], s3, r3,
                device_id=((z + d) % NZ, col), device_id_type=MESH,
            ).start()
        pltpu.make_async_copy(mine.at[0:5], mine.at[0:5], r3).wait()

    @pl.when(jnp.logical_not(reduces))
    def _():
        pltpu.make_async_copy(mine.at[0:6], mine.at[0:6], r3).wait()

    all_ref[core, chip] = mine[...]
    x, y = chip // 4, chip % 4
    steps = [(dx, dy) for dx in range(4) for dy in range(4) if dx or dy]
    steps.sort(key=lambda d: min(d[0], 4 - d[0]) + min(d[1], 4 - d[1]), reverse=True)
    for n, (dx, dy) in enumerate(steps):
        to = (((x + dx) % 4) * 4 + (y + dy) % 4) * 2 + core
        pltpu.make_async_remote_copy(
            mine, all_ref.at[core, chip], s4, r4.at[n], device_id=(z, to), device_id_type=MESH
        ).start()
    pltpu.make_async_remote_copy(
        mine, all_ref.at[core, chip], s5, r5, device_id=(z, sib), device_id_type=MESH
    ).start()
    for n, (dx, dy) in reversed(list(enumerate(steps))):
        source = ((x + 4 - dx) % 4) * 4 + (y + 4 - dy) % 4
        landed = all_ref.at[core, source]
        pltpu.make_async_copy(landed, landed, r4.at[n]).wait()
        pltpu.make_async_remote_copy(
            landed, landed, s5, r5, device_id=(z, sib), device_id_type=MESH
        ).start()
    other = all_ref.at[1 - core]
    pltpu.make_async_copy(other, other, r5).wait()

    pltpu.make_async_copy(other, other, s5).wait()
    pltpu.make_async_copy(all_ref.at[0, 0:15], all_ref.at[0, 0:15], s4).wait()

    @pl.when(reduces)
    def _():
        pltpu.make_async_copy(got2.at[0 : NZ - 1], got2.at[0 : NZ - 1], s3).wait()

    @pl.when(reduces)
    def _():
        pltpu.make_async_copy(got2.at[0 : NCH - 1], got2.at[0 : NCH - 1], s2).wait()

    @pl.when(jnp.logical_and(holds, core != turn))
    def _():
        pltpu.make_async_copy(got2.at[0:NCH], got2.at[0:NCH], s2).wait()

    @pl.when(is_x)
    def _():
        pltpu.make_async_copy(got2.at[0:18], got2.at[0:18], s1).wait()

    @pl.when(is_y)
    def _():
        pltpu.make_async_copy(got2.at[0:19], got2.at[0:19], s1).wait()

    @pl.when(jnp.logical_not(holds))
    def _():
        pltpu.make_async_copy(got2.at[0:20], got2.at[0:20], s1).wait()


def compute(own_ref, all_ref, inv_ref, factor_ref, next_ref, rhs, dexp, lhs, f1s, qqs, cross, solved, inv, outs):
    width = 2.0 * math.sqrt(2.0 * ND)
    lane = lax.broadcasted_iota(jnp.int32, (TR, TL), 1)
    low = lane < 64
    ones_lane = jnp.logical_and(lane >= 62, lane < 64)
    pad = NCH * PB

    rows_i = lax.broadcasted_iota(jnp.int32, (NCH * NC, pad), 0)
    cols_i = lax.broadcasted_iota(jnp.int32, (NCH * NC, pad), 1)
    block = cols_i // PB
    spread = jnp.where(
        jnp.logical_and(rows_i - block * NC == cols_i - block * PB, cols_i - block * PB < NC), 1.0, 0.0
    ).astype(BF16)
    inv[...] = dot(inv_ref[...], spread, NN).astype(BF16)

    def tile(j, kind, r):
        return all_ref[r % 2, j, kind * 2 + r // 2].astype(F32)

    def canon(y, odd):
        turned = pltpu.roll(y, 64, 1)
        return jnp.where(low, turned, y) if odd else jnp.where(low, y, turned)

    descs = []
    srows = []
    for j in range(NCH):
        sums = []
        for odd in range(2):
            base = TL * j + PB * odd
            for r in range(4):
                xt = tile(j, 2 if odd else 0, r)
                yt = tile(j, 1, r)
                keep = jnp.logical_and(lane >= 64, lane < 126) if odd else lane < 62
                rows = slice(base + TR * r, base + TR * r + TR)
                rhs[rows, 0:TL] = xt.astype(BF16)
                rhs[rows, TL : 2 * TL] = jnp.where(keep, yt, 0.0).astype(BF16)
                if j < NCH // 2:
                    lhs[rows, 0:TL] = xt.astype(BF16)
                    lhs[rows, TL : 2 * TL] = canon(yt, odd).astype(BF16)
                if r == 3:
                    d0 = xt[12:13, :]
                    d1 = canon(yt, odd)[12:13, :]
                    sums.append(xt[13:14, :] + xt[14:15, :])
                    descs.append((d0, d1))
            e0 = jnp.broadcast_to(d0, (TR, TL)).astype(BF16)
            e1 = jnp.broadcast_to(d1, (TR, TL))
            e1 = jnp.where(ones_lane, -1.0, jnp.where(low, e1, 0.0)).astype(BF16)
            for r in range(4):
                rows = slice(base + TR * r, base + TR * r + TR)
                dexp[rows, 0:TL] = e0
                dexp[rows, TL : 2 * TL] = e1
        srows.append(jnp.where(low[0:1], sums[0], sums[1]))
    srow = jnp.concatenate(srows, axis=1)

    for i in range(2):
        for r in range(4):
            rows = slice(NCH * PB + PB * i + TR * r, NCH * PB + PB * i + TR * r + TR)
            yt = canon(own_ref[8 + r].astype(F32), i)
            lhs[rows, 0:TL] = own_ref[2 * r + i]
            lhs[rows, TL : 2 * TL] = yt.astype(BF16)
            if r == 3:
                descs.append((own_ref[2 * r + i].astype(F32)[12:13, :], yt[12:13, :]))

    pick = list(range(NCH)) + [SLOTS, SLOTS + 1]
    zero_row = jnp.zeros((1, TL), F32)
    d0s = jnp.concatenate([descs[p][0] for p in pick] + [zero_row] * 6, axis=0)
    d1s = jnp.concatenate([descs[p][1] for p in pick] + [zero_row] * 6, axis=0)
    drows = jnp.concatenate([d0s, d1s], axis=1).astype(BF16)
    q = dot(drows, rhs[...], NT) - srow
    half = jnp.where(lax.broadcasted_iota(jnp.int32, (24, TL), 1) < 64, 1.0, 0.0)
    dists = []
    for j in range(NCH):
        cols = []
        for odd in range(2):
            u0 = d0s - descs[2 * j + odd][0]
            u1 = (d1s - descs[2 * j + odd][1]) * half
            cols.append(jnp.sum(u0 * u0 + u1 * u1, axis=1, keepdims=True))
        dists.append(jnp.where(half > 0.5, cols[0], cols[1]))
    dist = jnp.sqrt(jnp.concatenate(dists, axis=1))
    scaled = (math.sqrt(5.0) / width) * dist
    decay = jnp.exp(-scaled)
    f1s[...] = decay * (1.0 + scaled)
    qqs[...] = decay * (5.0 / (width * width)) * q

    own_lhs = lhs[pad : pad + TL, :]
    prod = dot(own_lhs, rhs[...], NT)
    prod2 = dot(own_lhs, dexp[...], NT)
    upper = lax.broadcasted_iota(jnp.int32, (TL, 1), 0) < PB
    f1 = jnp.where(upper, f1s[16:17, :], f1s[17:18, :])
    qq = jnp.where(upper, qqs[16:17, :], qqs[17:18, :])
    tiles = prod * f1 + prod2 * qq
    fresh = tiles[:, pad:]
    factor = dot(tiles[:, 0:pad].astype(BF16), inv[...], NT)
    outs[0:NC, :] = factor[0:NC, :]
    outs[NC : 2 * NC, :] = factor[PB : PB + NC, :]
    factor_ref[...] = outs[...].astype(BF16)

    @pl.loop(0, 4)
    def _(g):
        rows = pl.ds(pl.multiple_of(g * 256, 256), 256)
        part = lhs[rows, :]
        a = dot(part, rhs[pad:, :], NT)
        b = dot(part, dexp[pad:, :], NT)
        for i in range(4):
            f1_row = f1s[pl.ds(g * 4 + i, 1), pad:]
            qq_row = qqs[pl.ds(g * 4 + i, 1), pad:]
            got = a[PB * i : PB * i + PB, :] * f1_row + b[PB * i : PB * i + PB, :] * qq_row
            cross[pl.ds(pl.multiple_of(g * 256 + PB * i, PB), PB), :] = got.astype(BF16)

    @pl.loop(0, 3)
    def _(g):
        rows = pl.ds(pl.multiple_of(g * 320, 320), 320)
        solved[rows, :] = dot(inv[rows, :], cross[...], NN).astype(BF16)

    updated = (fresh - dot(factor.astype(BF16), solved[...], NN)).astype(BF16)
    final = dot(updated, spread, NT)
    outs[0:NC, :] = final[0:NC, :]
    outs[NC : 2 * NC, :] = final[PB : PB + NC, :]
    next_ref[...] = outs[...].astype(BF16)


VM = pl.BlockSpec(memory_space=pltpu.VMEM)
SM = pl.BlockSpec(memory_space=pltpu.SMEM)


def shards(jacobians, descriptors, block_inverse, tile_order, panel):
    own, everything = pl.pallas_call(
        exchange,
        name="exchange",
        out_shape=(
            jax.ShapeDtypeStruct((CHUNKS, TR, TL), BF16),
            jax.ShapeDtypeStruct((2, NCH, CHUNKS // 2, TR, TL), BF16),
        ),
        in_specs=[SM, SM, VM, VM],
        out_specs=(VM, VM),
        scratch_shapes=[
            pltpu.VMEM((2, PB, 2 * TL), F32),
            pltpu.VMEM((NZ, 2, TR, TL), BF16),
            pltpu.VMEM((NCH, TR, TL), BF16),
            pltpu.VMEM((2 * NCH, TR, TL), BF16),
            pltpu.VMEM((CHUNKS // 2, TR, TL), BF16),
            pltpu.SemaphoreType.DMA,
            pltpu.SemaphoreType.DMA,
            pltpu.SemaphoreType.DMA,
            pltpu.SemaphoreType.DMA,
            pltpu.SemaphoreType.DMA,
            pltpu.SemaphoreType.DMA,
            pltpu.SemaphoreType.DMA,
            pltpu.SemaphoreType.DMA((NCH - 1,)),
            pltpu.SemaphoreType.DMA,
            pltpu.SemaphoreType.DMA,
        ],
        compiler_params=pltpu.CompilerParams(
            collective_id=0, has_side_effects=True, vmem_limit_bytes=16 * 2**20
        ),
    )(tile_order, panel, jacobians, descriptors)
    pad = NCH * PB
    rows, pcols = jacobians.shape[0] * NC, block_inverse.shape[0]
    return pl.pallas_call(
        compute,
        name="compute",
        out_shape=(jax.ShapeDtypeStruct((rows, pcols), BF16),) * 2,
        in_specs=[VM, VM, VM],
        out_specs=(VM, VM),
        scratch_shapes=[
            pltpu.VMEM((2 * pad, 2 * TL), BF16),
            pltpu.VMEM((2 * pad, 2 * TL), BF16),
            pltpu.VMEM((pad + TL, 2 * TL), BF16),
            pltpu.VMEM((24, 2 * pad), F32),
            pltpu.VMEM((24, 2 * pad), F32),
            pltpu.VMEM((pad, pad), BF16),
            pltpu.VMEM((pcols, pad), BF16),
            pltpu.VMEM((pcols, pad), BF16),
            pltpu.VMEM((rows, pcols), F32),
        ],
        compiler_params=pltpu.CompilerParams(vmem_limit_bytes=48 * 2**20),
    )(own, everything, block_inverse)


def solution(mesh):
    placed = (P(("row", "col"), None, None), P(("row", "col"), None), P(), P(), P())
    return jax.shard_map(
        shards,
        mesh=mesh,
        in_specs=placed,
        out_specs=(P(("row", "col"), None), P(("row", "col"), None)),
        check_vma=False,
    )
```

```python
import functools
import math

import jax
import jax.numpy as jnp
from jax import lax
from jax.experimental import pallas as pl
from jax.experimental.pallas import tpu as pltpu
from jax.sharding import PartitionSpec as P

MESH = pl.DeviceIdType.MESH
F32 = jnp.float32
BF16 = jnp.bfloat16
NC = 60
ND = 190
PB = 64
TR = 16
TL = 128
NZ = 16
NCH = 16
NP = 32
SLOTS = 32
PCOLS = 960

NT = (((1,), (1,)), ((), ()))
NN = (((1,), (0,)), ((), ()))


def dot(a, b, dims):
    return lax.dot_general(a, b, dims, preferred_element_type=F32)


def iota(shape, dim):
    return lax.broadcasted_iota(jnp.int32, shape, dim)


def onehot(cond):
    return jnp.where(cond, 1.0, 0.0).astype(BF16)


def own_blocks(jac, desc_ref, blk, stage, send1, own_ref):
    lane = iota((1, TL), 1)
    low = lane < 64
    sums = jnp.logical_and(lane % 64 >= 62, lane >= 0)
    blk[...] = jnp.zeros_like(blk)
    stage[...] = jnp.zeros_like(stage)
    jac32 = jac[...].astype(F32)
    for i in range(2):
        one = jac32[:, i, :]
        desc32 = desc_ref[i : i + 1, :].astype(F32)
        col = jnp.sum(one * desc32, axis=1, keepdims=True)
        high = col.astype(BF16).astype(F32)
        blk[i, 0, 0:NC, :] = one[:, 0:TL]
        blk[i, 0, NC : NC + 1, :] = desc32[:, 0:TL]
        blk[i, 1, 0:NC, 0 : ND - TL] = one[:, TL:ND]
        blk[i, 1, 0:NC, ND - TL : ND - TL + 1] = high
        blk[i, 1, 0:NC, ND - TL + 1 : ND - TL + 2] = col - high
        blk[i, 1, NC : NC + 1, 0 : ND - TL] = desc32[:, TL:ND]
        rest = blk[i, 1]
        both = rest + pltpu.roll(rest, 64, 1)
        is_desc = iota((PB, TL), 0) == NC
        rows = slice(PB * i, PB * i + PB)
        own_ref[rows, 0:TL] = blk[i, 0].astype(BF16)
        own_ref[rows, TL : 2 * TL] = jnp.where(sums, jnp.where(is_desc, -1.0, 0.0), both).astype(BF16)
        own_ref[rows, 2 * TL : 3 * TL] = rest.astype(BF16)
        even = blk[i, 1, pl.ds(0, NP, stride=2), :]
        odd = blk[i, 1, pl.ds(1, NP, stride=2), :]
        pair = jnp.where(low, even, pltpu.roll(odd, 64, 1))
        for q in range(NP):
            stage[q, 2 * i : 2 * i + 2, :] = blk[i, 0, 2 * q : 2 * q + 2, :]
            stage[q, 4 + i : 5 + i, :] = pair[q : q + 1, :]
    for q in range(NP):
        send1[q] = stage[q].astype(BF16)


def choices(order, panel, z, cap, step, total, one1, one2, over_ref, fast):
    base = panel[0] * TR
    lane = iota((8, TL), 1)
    sub = iota((8, TL), 0)
    parts = []
    line = jnp.zeros((8, TL), jnp.int32)
    for g in range(SLOTS // 8):
        part = jnp.zeros((8, TL), jnp.int32)
        for s in range(8 * g, 8 * g + 8):
            conf = order[base + s]
            part = jnp.where(sub == s - 8 * g, conf, part)
            line = jnp.where(lane == s, conf, line)
        parts.append(part)
    conf_col = jnp.concatenate(parts, axis=0)
    conf_row = jnp.concatenate([line] * 4, axis=0)
    plane_col = conf_col // (2 * NP)
    plane_row = conf_row // (2 * NP)
    slot_col = iota((SLOTS, TL), 0)
    slot_row = iota((SLOTS, TL), 1)
    same = plane_col == plane_row
    before = jnp.logical_and(same, slot_row < slot_col)
    rank_col = jnp.sum(jnp.where(before, 1.0, 0.0), axis=1, keepdims=True)
    if over_ref is not None:
        over_ref[0] = jnp.where(jnp.max(rank_col) >= cap, 1, 0)
    rank_col = jnp.broadcast_to(rank_col, (SLOTS, TL)).astype(jnp.int32)
    place = rank_col if fast else slot_col
    here = plane_col == z
    device = (conf_col // 2) % NP
    which = conf_col % 2
    finds = []
    for kind in range(3):
        at = device * TR + (2 * which + kind if kind < 2 else 4 + which)
        find = []
        for t in range(NP * TR // TL):
            find.append(jnp.logical_and(at == slot_row + TL * t, here))
        finds.append(onehot(jnp.concatenate(find, axis=1)))
        goal = plane_col * total + kind * step + place
        take = [goal == slot_row + TL * t for t in range(NZ * total // TL)]
        one2[kind * SLOTS : kind * SLOTS + SLOTS, :] = onehot(jnp.concatenate(take, axis=1))
    finds = jnp.concatenate(finds, axis=0)
    if fast:
        after = jnp.logical_and(same, slot_col < slot_row)
        rank_row = jnp.sum(jnp.where(after, 1.0, 0.0), axis=0, keepdims=True).astype(jnp.int32)
        row = iota((total, SLOTS), 0)
        packs = []
        for kind in range(3):
            here_row = plane_row[0:1, 0:SLOTS] == z
            hit = jnp.logical_and(row == kind * step + rank_row[:, 0:SLOTS], rank_row[:, 0:SLOTS] < cap)
            packs.append(jnp.where(jnp.logical_and(hit, here_row), 1.0, 0.0))
        pack = jnp.concatenate(packs, axis=1).astype(BF16)
        one1[...] = dot(pack, finds, NN).astype(BF16)
    else:
        one1[...] = finds


def exchange(cap, step, total, fast, *refs):
    order_ref, panel_ref, jac_ref, desc_ref, inv_ref = refs[:5]
    if fast:
        own_ref, all_ref, inv_out, perm_out, over_ref = refs[5:10]
        rest = refs[10:]
    else:
        own_ref, all_ref = refs[5:7]
        inv_out = perm_out = over_ref = None
        rest = refs[7:]
    (order, panel, jac, desc, inv, blk, stage, send1, got1, one1, send2, got2, one2, mine, ins,
     s1, r1, s2, r2, s4, r4, s5, r5) = rest
    z = lax.axis_index("row")
    col = lax.axis_index("col")
    core = col % 2
    chip = col // 2
    sib = chip * 2 + 1 - core

    barrier = pltpu.get_barrier_semaphore()
    far = sorted(range(1, NZ), key=lambda d: -min(d, NZ - d))
    for d in far:
        pl.semaphore_signal(barrier, inc=1, device_id=((z + d) % NZ, col), device_id_type=MESH)
    for d in range(1, NP):
        pl.semaphore_signal(barrier, inc=1, device_id=(z, (col + d) % NP), device_id_type=MESH)
    loads = [(jac_ref, jac), (desc_ref, desc), (order_ref, order), (panel_ref, panel)]
    if fast:
        loads.append((inv_ref, inv))
    loads = [pltpu.make_async_copy(a, b, ins.at[n]) for n, (a, b) in enumerate(loads)]
    for load in loads:
        load.start()
    loads[0].wait()
    loads[1].wait()
    own_blocks(jac, desc, blk, stage, send1, own_ref)
    pl.semaphore_wait(barrier, NZ - 1 + NP - 1)

    for d in range(1, NP):
        to = (col + d) % NP
        pltpu.make_async_remote_copy(
            send1.at[to], got1.at[col], s1, r1, device_id=(z, to), device_id_type=MESH
        ).start()
    got1[col] = send1[col]
    loads[2].wait()
    loads[3].wait()
    choices(order, panel, z, cap, step, total, one1, one2, over_ref, fast)
    if fast:
        at = iota((PCOLS, PCOLS), 1)
        perm_out[...] = onehot(iota((PCOLS, PCOLS), 0) == (at % TR) * NC + at // TR)
        loads[4].wait()
    pltpu.make_async_copy(got1.at[0 : NP - 1], got1.at[0 : NP - 1], r1).wait()

    send2[...] = dot(one1[...], got1[...].reshape(NP * TR, TL), NN).astype(BF16)
    for d in far:
        pltpu.make_async_remote_copy(
            send2, got2.at[z], s2, r2, device_id=((z + d) % NZ, col), device_id_type=MESH
        ).start()
    got2[z] = send2[...]
    if fast:

        @pl.loop(0, 3)
        def _(g):
            rows = pl.ds(pl.multiple_of(g * 320, 320), 320)
            inv_out[rows, :] = dot(inv[rows, :], perm_out[...], NN).astype(BF16)

    pltpu.make_async_copy(got2.at[0 : NZ - 1], got2.at[0 : NZ - 1], r2).wait()
    mine[...] = dot(one2[...], got2[...].reshape(NZ * total, TL), NN).astype(BF16)

    x, y = chip // 4, chip % 4
    steps = [(dx, dy) for dx in range(4) for dy in range(4) if dx or dy]
    steps.sort(key=lambda d: min(d[0], 4 - d[0]) + min(d[1], 4 - d[1]), reverse=True)
    for n, (dx, dy) in enumerate(steps):
        to = (((x + dx) % 4) * 4 + (y + dy) % 4) * 2 + core
        pltpu.make_async_remote_copy(
            mine, all_ref.at[core, chip], s4, r4.at[n], device_id=(z, to), device_id_type=MESH
        ).start()
    pltpu.make_async_remote_copy(
        mine, all_ref.at[core, chip], s5, r5, device_id=(z, sib), device_id_type=MESH
    ).start()
    all_ref[core, chip] = mine[...]
    for n, (dx, dy) in reversed(list(enumerate(steps))):
        source = ((x + 4 - dx) % 4) * 4 + (y + 4 - dy) % 4
        landed = all_ref.at[core, source]
        pltpu.make_async_copy(landed, landed, r4.at[n]).wait()
        pltpu.make_async_remote_copy(
            landed, landed, s5, r5, device_id=(z, sib), device_id_type=MESH
        ).start()
    other = all_ref.at[1 - core]
    pltpu.make_async_copy(other, other, r5).wait()

    pltpu.make_async_copy(got1.at[0 : NP - 1], got1.at[0 : NP - 1], s1).wait()
    pltpu.make_async_copy(got2.at[0 : NZ - 1], got2.at[0 : NZ - 1], s2).wait()
    pltpu.make_async_copy(all_ref.at[0, 0:15], all_ref.at[0, 0:15], s4).wait()
    pltpu.make_async_copy(other, other, s5).wait()


def compute(own_ref, all_ref, inv_ref, perm_ref, factor_ref, next_ref, rhs, lhs, lhs2, dexp, cross, solved, outs):
    width = 2.0 * math.sqrt(2.0 * ND)
    lane = iota((TR, TL), 1)
    low = lane < 64
    sums = lane % 64 >= 62
    last = jnp.logical_and(lane >= 62, low)

    def piece(row, kind, half):
        p = row // 2
        first = (kind * 2 + half) * TR
        return all_ref[p % 2, p // 2, first : first + TR, :]

    ds = []
    for half in range(2):
        for p in range(NC // 2 + 1):
            rest = piece(2 * p, 2, half).astype(F32)
            turned = pltpu.roll(rest, 64, 1)
            for odd in range(2):
                row = 2 * p + odd
                if row > NC:
                    continue
                xt = piece(row, odd, half)
                rows = slice(TR * row, TR * row + TR)
                mine = turned if odd else rest
                if row < NC:
                    rhs[half, rows, 0:TL] = xt
                    rhs[half, rows, TL : 2 * TL] = jnp.where(low != (odd == 1), rest, 0.0).astype(BF16)
                if half == 0:
                    both = jnp.where(low != (odd == 1), rest, turned)
                    lhs[rows, 0:TL] = xt
                    lhs[rows, TL : 2 * TL] = jnp.where(sums, -1.0 if row == NC else 0.0, both).astype(BF16)
                    if row < NC:
                        lhs2[rows, 0:TL] = xt
                        lhs2[rows, TL : 2 * TL] = mine.astype(BF16)
                if row == NC:
                    d0, d1 = xt.astype(F32), jnp.where(low, rest, 0.0)
                    ds.append((d0, d1))
                    e1 = jnp.where(last, -1.0, d1).astype(BF16)
                    for t in range(TL // TR):
                        to = slice(TL * half + TR * t, TL * half + TR * t + TR)
                        dexp[to, 0:TL] = xt
                        dexp[to, TL : 2 * TL] = e1

    zero = jnp.zeros((6, TL), F32)
    own_d = [own_ref[PB * i + NC - 12 : PB * i + PB - 0, :].astype(F32)[12:13] for i in range(2)]
    d0s = jnp.concatenate([ds[0][0]] + [d[:, 0:TL] for d in own_d] + [zero], axis=0)
    d1s = jnp.concatenate([ds[0][1]] + [jnp.where(low[0:1], d[:, 2 * TL :], 0.0) for d in own_d] + [zero], axis=0)
    f1s, f2s = [], []
    lane24 = iota((24, TL), 1) % TR
    for half in range(2):
        dist = jnp.zeros((24, TL), F32)
        for b in range(TR):
            u0 = d0s - ds[half][0][b : b + 1, :]
            u1 = d1s - ds[half][1][b : b + 1, :]
            dist = jnp.where(lane24 == b, jnp.sum(u0 * u0 + u1 * u1, axis=1, keepdims=True), dist)
        scaled = (math.sqrt(5.0) / width) * jnp.sqrt(dist)
        decay = jnp.exp(-scaled)
        f1s.append(decay * (1.0 + scaled))
        f2s.append(decay * (5.0 / (width * width)))

    def wide(tile):
        return jnp.concatenate([tile] * 8, axis=1)[:, 0:PCOLS]

    own_lhs = own_ref[:, 0 : 2 * TL]
    own_lhs2 = jnp.concatenate([own_ref[:, 0:TL], own_ref[:, 2 * TL :]], axis=1)
    prod2 = dot(own_lhs2, dexp[...], NT)
    tiles = []
    for half in range(2):
        prod = dot(own_lhs, rhs[half], NT)
        parts = []
        for i in range(2):
            rows = slice(PB * i, PB * i + PB)
            f1 = wide(f1s[half][TR + i : TR + i + 1, :])
            qq = wide(f2s[half][TR + i : TR + i + 1, :]) * prod[PB * i + NC : PB * i + NC + 1, :]
            p = wide(prod2[rows, TL * half : TL * half + TL])
            parts.append(prod[rows, :] * f1 + p * qq)
        tiles.append(jnp.concatenate(parts, axis=0))
    factor = dot(tiles[0].astype(BF16), inv_ref[...], NT)
    outs[0:NC, :] = factor[0:NC, :]
    outs[NC : 2 * NC, :] = factor[PB : PB + NC, :]
    factor_ref[...] = outs[...].astype(BF16)

    qq = wide(f2s[1][0:TR, :]) * dot(lhs[PCOLS : PCOLS + TR, :], rhs[1], NT)
    f1 = wide(f1s[1][0:TR, :])

    @pl.loop(0, 4)
    def _(g):
        rows = pl.ds(pl.multiple_of(g * 240, 240), 240)
        a = dot(lhs[rows, :], rhs[1], NT)
        b = dot(lhs2[rows, :], dexp[TL : 2 * TL, :], NT)
        got = []
        for n in range(15):
            part = slice(TR * n, TR * n + TR)
            got.append((a[part, :] * f1 + wide(b[part, :]) * qq).astype(BF16))
        cross[rows, :] = jnp.concatenate(got, axis=0)

    @pl.loop(0, 3)
    def _(g):
        rows = pl.ds(pl.multiple_of(g * 320, 320), 320)
        solved[rows, :] = dot(inv_ref[rows, :], cross[...], NN).astype(BF16)

    updated = (tiles[1] - dot(factor.astype(BF16), solved[...], NN)).astype(BF16)
    final = dot(updated, perm_ref[...], NT)
    outs[0:NC, :] = final[0:NC, :]
    outs[NC : 2 * NC, :] = final[PB : PB + NC, :]
    next_ref[...] = outs[...].astype(BF16)


VM = pl.BlockSpec(memory_space=pltpu.VMEM)
ANY = pl.BlockSpec(memory_space=pl.ANY)


def run_exchange(fast, order, panel, jac, desc, inv):
    cap, step, total = (10, 10, 32) if fast else (32, 32, 96)
    square = jax.ShapeDtypeStruct((PCOLS, PCOLS), BF16)
    outs = (
        jax.ShapeDtypeStruct((2 * PB, 3 * TL), BF16),
        jax.ShapeDtypeStruct((2, NCH, 3 * SLOTS, TL), BF16),
    )
    specs = (VM, VM)
    if fast:
        outs += (square, square, jax.ShapeDtypeStruct((1,), jnp.int32))
        specs += (VM, VM, pl.BlockSpec(memory_space=pltpu.SMEM))
    dma = pltpu.SemaphoreType.DMA
    return pl.pallas_call(
        functools.partial(exchange, cap, step, total, fast),
        name="exchange" if fast else "exchange_full",
        out_shape=outs,
        in_specs=[ANY] * 5,
        out_specs=specs,
        scratch_shapes=[
            pltpu.SMEM((NZ * 2 * NP,), jnp.int32),
            pltpu.SMEM((1,), jnp.int32),
            pltpu.VMEM(jac.shape, BF16),
            pltpu.VMEM(desc.shape, BF16),
            pltpu.VMEM((PCOLS, PCOLS) if fast else (TR, TL), BF16),
            pltpu.VMEM((2, 2, PB, TL), F32),
            pltpu.VMEM((NP, TR, TL), F32),
            pltpu.VMEM((NP, TR, TL), BF16),
            pltpu.VMEM((NP, TR, TL), BF16),
            pltpu.VMEM((total, NP * TR), BF16),
            pltpu.VMEM((total, TL), BF16),
            pltpu.VMEM((NZ, total, TL), BF16),
            pltpu.VMEM((3 * SLOTS, NZ * total), BF16),
            pltpu.VMEM((3 * SLOTS, TL), BF16),
            dma((5,)), dma, dma, dma, dma, dma, dma((NCH - 1,)), dma, dma,
        ],
        compiler_params=pltpu.CompilerParams(
            collective_id=0 if fast else 1, has_side_effects=True, vmem_limit_bytes=24 * 2**20
        ),
    )(order, panel, jac, desc, inv)


def run_compute(own, everything, inv, perm):
    rows = 2 * NC
    return pl.pallas_call(
        compute,
        name="compute",
        out_shape=(jax.ShapeDtypeStruct((rows, PCOLS), BF16),) * 2,
        in_specs=[VM] * 4,
        out_specs=(VM, VM),
        scratch_shapes=[
            pltpu.VMEM((2, PCOLS, 2 * TL), BF16),
            pltpu.VMEM((PCOLS + TR, 2 * TL), BF16),
            pltpu.VMEM((PCOLS, 2 * TL), BF16),
            pltpu.VMEM((2 * TL, 2 * TL), BF16),
            pltpu.VMEM((PCOLS, PCOLS), BF16),
            pltpu.VMEM((PCOLS, PCOLS), BF16),
            pltpu.VMEM((rows, PCOLS), F32),
        ],
        compiler_params=pltpu.CompilerParams(vmem_limit_bytes=40 * 2**20),
    )(own, everything, inv, perm)


def shards(jacobians, descriptors, block_inverse, tile_order, panel):
    jac = jnp.transpose(jacobians, (1, 0, 2))
    args = (tile_order, panel, jac, descriptors, block_inverse)
    own, few, inv, perm, over = run_exchange(True, *args)

    def usual():
        return run_compute(own, few, inv, perm)

    def crowded():
        again, everything = run_exchange(False, *args)
        return run_compute(again, everything, inv, perm)

    return lax.cond(over[0] == 0, usual, crowded)


def solution(mesh):
    placed = (P(("row", "col"), None, None), P(("row", "col"), None), P(), P(), P())
    return jax.shard_map(
        shards,
        mesh=mesh,
        in_specs=placed,
        out_specs=(P(("row", "col"), None), P(("row", "col"), None)),
        check_vma=False,
    )
```

```python
import functools
import math

import jax
import jax.numpy as jnp
from jax import lax
from jax.experimental import pallas as pl
from jax.experimental.pallas import tpu as pltpu
from jax.sharding import PartitionSpec as P

MESH = pl.DeviceIdType.MESH
F32 = jnp.float32
BF16 = jnp.bfloat16
NC = 60
ND = 190
PB = 64
TR = 16
TL = 128
NZ = 16
NCH = 16
NP = 32
SLOTS = 32
PCOLS = 960

NT = (((1,), (1,)), ((), ()))
NN = (((1,), (0,)), ((), ()))


def dot(a, b, dims):
    return lax.dot_general(a, b, dims, preferred_element_type=F32)


def iota(shape, dim):
    return lax.broadcasted_iota(jnp.int32, shape, dim)


def onehot(cond):
    return jnp.where(cond, 1.0, 0.0).astype(BF16)


def own_blocks(jac, desc_ref, blk, stage, send1, own_ref):
    lane = iota((1, TL), 1)
    low = lane < 64
    sums = jnp.logical_and(lane % 64 >= 62, lane >= 0)
    blk[...] = jnp.zeros_like(blk)
    stage[...] = jnp.zeros_like(stage)
    jac32 = jac[...].astype(F32)
    for i in range(2):
        one = jac32[:, i, :]
        desc32 = desc_ref[i : i + 1, :].astype(F32)
        col = jnp.sum(one * desc32, axis=1, keepdims=True)
        high = col.astype(BF16).astype(F32)
        blk[i, 0, 0:NC, :] = one[:, 0:TL]
        blk[i, 0, NC : NC + 1, :] = desc32[:, 0:TL]
        blk[i, 1, 0:NC, 0 : ND - TL] = one[:, TL:ND]
        blk[i, 1, 0:NC, ND - TL : ND - TL + 1] = high
        blk[i, 1, 0:NC, ND - TL + 1 : ND - TL + 2] = col - high
        blk[i, 1, NC : NC + 1, 0 : ND - TL] = desc32[:, TL:ND]
        rest = blk[i, 1]
        both = rest + pltpu.roll(rest, 64, 1)
        is_desc = iota((PB, TL), 0) == NC
        rows = slice(PB * i, PB * i + PB)
        own_ref[rows, 0:TL] = blk[i, 0].astype(BF16)
        own_ref[rows, TL : 2 * TL] = jnp.where(sums, jnp.where(is_desc, -1.0, 0.0), both).astype(BF16)
        own_ref[rows, 2 * TL : 3 * TL] = rest.astype(BF16)
        even = blk[i, 1, pl.ds(0, NP, stride=2), :]
        odd = blk[i, 1, pl.ds(1, NP, stride=2), :]
        pair = jnp.where(low, even, pltpu.roll(odd, 64, 1))
        for q in range(NP):
            stage[q, 2 * i : 2 * i + 2, :] = blk[i, 0, 2 * q : 2 * q + 2, :]
            stage[q, 4 + i : 5 + i, :] = pair[q : q + 1, :]
    for q in range(NP):
        send1[q] = stage[q].astype(BF16)


def choices(order, panel, z, cap, step, total, one1, one2, over_ref, fast):
    base = panel[0] * TR
    lane = iota((8, TL), 1)
    sub = iota((8, TL), 0)
    parts = []
    line = jnp.zeros((8, TL), jnp.int32)
    for g in range(SLOTS // 8):
        part = jnp.zeros((8, TL), jnp.int32)
        for s in range(8 * g, 8 * g + 8):
            conf = order[base + s]
            part = jnp.where(sub == s - 8 * g, conf, part)
            line = jnp.where(lane == s, conf, line)
        parts.append(part)
    conf_col = jnp.concatenate(parts, axis=0)
    conf_row = jnp.concatenate([line] * 4, axis=0)
    plane_col = conf_col // (2 * NP)
    plane_row = conf_row // (2 * NP)
    slot_col = iota((SLOTS, TL), 0)
    slot_row = iota((SLOTS, TL), 1)
    same = plane_col == plane_row
    before = jnp.logical_and(same, slot_row < slot_col)
    rank_col = jnp.sum(jnp.where(before, 1.0, 0.0), axis=1, keepdims=True)
    if over_ref is not None:
        over_ref[0] = jnp.where(jnp.max(rank_col) >= cap, 1, 0)
    rank_col = jnp.broadcast_to(rank_col, (SLOTS, TL)).astype(jnp.int32)
    place = rank_col if fast else slot_col
    here = plane_col == z
    device = (conf_col // 2) % NP
    which = conf_col % 2
    finds = []
    for kind in range(3):
        at = device * TR + (2 * which + kind if kind < 2 else 4 + which)
        find = []
        for t in range(NP * TR // TL):
            find.append(jnp.logical_and(at == slot_row + TL * t, here))
        finds.append(onehot(jnp.concatenate(find, axis=1)))
        goal = plane_col * total + kind * step + place
        take = [goal == slot_row + TL * t for t in range(NZ * total // TL)]
        one2[kind * SLOTS : kind * SLOTS + SLOTS, :] = onehot(jnp.concatenate(take, axis=1))
    finds = jnp.concatenate(finds, axis=0)
    if fast:
        after = jnp.logical_and(same, slot_col < slot_row)
        rank_row = jnp.sum(jnp.where(after, 1.0, 0.0), axis=0, keepdims=True).astype(jnp.int32)
        row = iota((total, SLOTS), 0)
        packs = []
        for kind in range(3):
            here_row = plane_row[0:1, 0:SLOTS] == z
            hit = jnp.logical_and(row == kind * step + rank_row[:, 0:SLOTS], rank_row[:, 0:SLOTS] < cap)
            packs.append(jnp.where(jnp.logical_and(hit, here_row), 1.0, 0.0))
        pack = jnp.concatenate(packs, axis=1).astype(BF16)
        one1[...] = dot(pack, finds, NN).astype(BF16)
    else:
        one1[...] = finds


def exchange(cap, step, total, fast, *refs):
    order_ref, panel_ref, jac_ref, desc_ref, inv_ref = refs[:5]
    if fast:
        own_ref, all_ref, inv_out, perm_out, over_ref = refs[5:10]
        rest = refs[10:]
    else:
        own_ref, all_ref = refs[5:7]
        inv_out = perm_out = over_ref = None
        rest = refs[7:]
    (order, panel, jac, desc, inv, blk, stage, send1, got1, one1, send2, got2, one2, mine, ins,
     s1, r1, s2, r2, s4, r4, s5, r5) = rest
    z = lax.axis_index("row")
    col = lax.axis_index("col")
    core = col % 2
    chip = col // 2
    sib = chip * 2 + 1 - core

    barrier = pltpu.get_barrier_semaphore()
    far = sorted(range(1, NZ), key=lambda d: -min(d, NZ - d))
    for d in far:
        pl.semaphore_signal(barrier, inc=1, device_id=((z + d) % NZ, col), device_id_type=MESH)
    for d in range(1, NP):
        pl.semaphore_signal(barrier, inc=1, device_id=(z, (col + d) % NP), device_id_type=MESH)
    loads = [(jac_ref, jac), (desc_ref, desc), (order_ref, order), (panel_ref, panel)]
    if fast:
        loads.append((inv_ref, inv))
    loads = [pltpu.make_async_copy(a, b, ins.at[n]) for n, (a, b) in enumerate(loads)]
    for load in loads:
        load.start()
    loads[0].wait()
    loads[1].wait()
    own_blocks(jac, desc, blk, stage, send1, own_ref)
    pl.semaphore_wait(barrier, NZ - 1 + NP - 1)

    for d in range(1, NP):
        to = (col + d) % NP
        pltpu.make_async_remote_copy(
            send1.at[to], got1.at[col], s1, r1, device_id=(z, to), device_id_type=MESH
        ).start()
    got1[col] = send1[col]
    loads[2].wait()
    loads[3].wait()
    choices(order, panel, z, cap, step, total, one1, one2, over_ref, fast)
    if fast:
        at = iota((PCOLS, PCOLS), 1)
        perm_out[...] = onehot(iota((PCOLS, PCOLS), 0) == (at % TR) * NC + at // TR)
        loads[4].wait()
    pltpu.make_async_copy(got1.at[0 : NP - 1], got1.at[0 : NP - 1], r1).wait()

    send2[...] = dot(one1[...], got1[...].reshape(NP * TR, TL), NN).astype(BF16)
    for d in far:
        pltpu.make_async_remote_copy(
            send2, got2.at[z], s2, r2, device_id=((z + d) % NZ, col), device_id_type=MESH
        ).start()
    got2[z] = send2[...]
    if fast:

        @pl.loop(0, 3)
        def _(g):
            rows = pl.ds(pl.multiple_of(g * 320, 320), 320)
            inv_out[rows, :] = dot(inv[rows, :], perm_out[...], NN).astype(BF16)

    pltpu.make_async_copy(got2.at[0 : NZ - 1], got2.at[0 : NZ - 1], r2).wait()
    mine[...] = dot(one2[...], got2[...].reshape(NZ * total, TL), NN).astype(BF16)

    x, y = chip // 4, chip % 4
    steps = [(dx, dy) for dx in range(4) for dy in range(4) if dx or dy]
    steps.sort(key=lambda d: min(d[0], 4 - d[0]) + min(d[1], 4 - d[1]), reverse=True)
    for n, (dx, dy) in enumerate(steps):
        to = (((x + dx) % 4) * 4 + (y + dy) % 4) * 2 + core
        pltpu.make_async_remote_copy(
            mine, all_ref.at[core, chip], s4, r4.at[n], device_id=(z, to), device_id_type=MESH
        ).start()
    pltpu.make_async_remote_copy(
        mine, all_ref.at[core, chip], s5, r5, device_id=(z, sib), device_id_type=MESH
    ).start()
    all_ref[core, chip] = mine[...]
    for n, (dx, dy) in reversed(list(enumerate(steps))):
        source = ((x + 4 - dx) % 4) * 4 + (y + 4 - dy) % 4
        landed = all_ref.at[core, source]
        pltpu.make_async_copy(landed, landed, r4.at[n]).wait()
        pltpu.make_async_remote_copy(
            landed, landed, s5, r5, device_id=(z, sib), device_id_type=MESH
        ).start()
    other = all_ref.at[1 - core]
    pltpu.make_async_copy(other, other, r5).wait()

    pltpu.make_async_copy(got1.at[0 : NP - 1], got1.at[0 : NP - 1], s1).wait()
    pltpu.make_async_copy(got2.at[0 : NZ - 1], got2.at[0 : NZ - 1], s2).wait()
    pltpu.make_async_copy(all_ref.at[0, 0:15], all_ref.at[0, 0:15], s4).wait()
    pltpu.make_async_copy(other, other, s5).wait()


def compute(own_ref, all_ref, inv_ref, perm_ref, factor_ref, next_ref, rhs, lhs, lhs2, dexp, cross, outs):
    width = 2.0 * math.sqrt(2.0 * ND)
    lane = iota((TR, TL), 1)
    low = lane < 64
    sums = lane % 64 >= 62
    last = jnp.logical_and(lane >= 62, low)

    def piece(row, kind, half):
        p = row // 2
        first = (kind * 2 + half) * TR
        return all_ref[p % 2, p // 2, first : first + TR, :]

    ds = []
    for half in range(2):
        for p in range(NC // 2 + 1):
            rest = piece(2 * p, 2, half).astype(F32)
            turned = pltpu.roll(rest, 64, 1)
            for odd in range(2):
                row = 2 * p + odd
                if row > NC:
                    continue
                xt = piece(row, odd, half)
                rows = slice(TR * row, TR * row + TR)
                mine = turned if odd else rest
                if row < NC:
                    rhs[half, rows, 0:TL] = xt
                    rhs[half, rows, TL : 2 * TL] = jnp.where(low != (odd == 1), rest, 0.0).astype(BF16)
                if half == 0:
                    both = jnp.where(low != (odd == 1), rest, turned)
                    lhs[rows, 0:TL] = xt
                    lhs[rows, TL : 2 * TL] = jnp.where(sums, -1.0 if row == NC else 0.0, both).astype(BF16)
                    if row < NC:
                        lhs2[rows, 0:TL] = xt
                        lhs2[rows, TL : 2 * TL] = mine.astype(BF16)
                if row == NC:
                    d0, d1 = xt.astype(F32), jnp.where(low, rest, 0.0)
                    ds.append((d0, d1))
                    e1 = jnp.where(last, -1.0, d1).astype(BF16)
                    for t in range(TL // TR):
                        to = slice(TL * half + TR * t, TL * half + TR * t + TR)
                        dexp[to, 0:TL] = xt
                        dexp[to, TL : 2 * TL] = e1

    zero = jnp.zeros((6, TL), F32)
    own_d = [own_ref[PB * i + NC - 12 : PB * i + PB - 0, :].astype(F32)[12:13] for i in range(2)]
    d0s = jnp.concatenate([ds[0][0]] + [d[:, 0:TL] for d in own_d] + [zero], axis=0)
    d1s = jnp.concatenate([ds[0][1]] + [jnp.where(low[0:1], d[:, 2 * TL :], 0.0) for d in own_d] + [zero], axis=0)
    f1s, f2s = [], []
    lane24 = iota((24, TL), 1) % TR
    for half in range(2):
        dist = jnp.zeros((24, TL), F32)
        for b in range(TR):
            u0 = d0s - ds[half][0][b : b + 1, :]
            u1 = d1s - ds[half][1][b : b + 1, :]
            dist = jnp.where(lane24 == b, jnp.sum(u0 * u0 + u1 * u1, axis=1, keepdims=True), dist)
        scaled = (math.sqrt(5.0) / width) * jnp.sqrt(dist)
        decay = jnp.exp(-scaled)
        f1s.append(decay * (1.0 + scaled))
        f2s.append(decay * (5.0 / (width * width)))

    def wide(tile):
        return jnp.concatenate([tile] * 8, axis=1)[:, 0:PCOLS]

    own_lhs = own_ref[:, 0 : 2 * TL]
    own_lhs2 = jnp.concatenate([own_ref[:, 0:TL], own_ref[:, 2 * TL :]], axis=1)
    prod2 = dot(own_lhs2, dexp[...], NT)
    tiles = []
    for half in range(2):
        prod = dot(own_lhs, rhs[half], NT)
        parts = []
        for i in range(2):
            rows = slice(PB * i, PB * i + PB)
            f1 = wide(f1s[half][TR + i : TR + i + 1, :])
            qq = wide(f2s[half][TR + i : TR + i + 1, :]) * prod[PB * i + NC : PB * i + NC + 1, :]
            p = wide(prod2[rows, TL * half : TL * half + TL])
            parts.append(prod[rows, :] * f1 + p * qq)
        tiles.append(jnp.concatenate(parts, axis=0))
    factor = dot(tiles[0].astype(BF16), inv_ref[...], NT)
    outs[0:NC, :] = factor[0:NC, :]
    outs[NC : 2 * NC, :] = factor[PB : PB + NC, :]
    factor_ref[...] = outs[...].astype(BF16)
    most = jnp.max(jnp.abs(factor), axis=1, keepdims=True)
    scale = jnp.ones_like(most)
    back = jnp.ones_like(most)
    for _ in range(4):
        large = most * scale > 2.0**24
        scale = jnp.where(large, scale * 2.0**-24, scale)
        back = jnp.where(large, back * 2.0**24, back)
    scaled_factor = (factor.astype(BF16).astype(F32) * scale).astype(BF16)

    qq = wide(f2s[1][0:TR, :]) * dot(lhs[PCOLS : PCOLS + TR, :], rhs[1], NT)
    f1 = wide(f1s[1][0:TR, :])

    for g in range(4):
        rows = slice(240 * g, 240 * g + 240)
        a = dot(lhs[rows, :], rhs[1], NT)
        b = dot(lhs2[rows, :], dexp[TL : 2 * TL, :], NT)
        got = []
        for n in range(15):
            part = slice(TR * n, TR * n + TR)
            got.append((a[part, :] * f1 + wide(b[part, :]) * qq).astype(BF16))
        cross[rows, :] = jnp.concatenate(got, axis=0)

    middle = dot(scaled_factor, inv_ref[...], NN)
    high = middle.astype(BF16)
    both = jnp.concatenate([high, (middle - high.astype(F32)).astype(BF16)], axis=0)
    change = dot(both, cross[...], NN)
    change = (change[0:TL, :] + change[TL : 2 * TL, :]) * back
    updated = (tiles[1] - change).astype(BF16)
    final = dot(updated, perm_ref[...], NT)
    outs[0:NC, :] = final[0:NC, :]
    outs[NC : 2 * NC, :] = final[PB : PB + NC, :]
    next_ref[...] = outs[...].astype(BF16)


VM = pl.BlockSpec(memory_space=pltpu.VMEM)
HBM = pl.BlockSpec(memory_space=pltpu.HBM)


def run_exchange(fast, order, panel, jac, desc, inv):
    cap, step, total = (10, 10, 32) if fast else (32, 32, 96)
    square = jax.ShapeDtypeStruct((PCOLS, PCOLS), BF16)
    outs = (
        jax.ShapeDtypeStruct((2 * PB, 3 * TL), BF16),
        jax.ShapeDtypeStruct((2, NCH, 3 * SLOTS, TL), BF16),
    )
    specs = (VM, VM)
    if fast:
        outs += (square, square, jax.ShapeDtypeStruct((1,), jnp.int32))
        specs += (VM, VM, pl.BlockSpec(memory_space=pltpu.SMEM))
    dma = pltpu.SemaphoreType.DMA
    return pl.pallas_call(
        functools.partial(exchange, cap, step, total, fast),
        name="exchange" if fast else "exchange_full",
        out_shape=outs,
        in_specs=[HBM] * 5,
        out_specs=specs,
        scratch_shapes=[
            pltpu.SMEM((NZ * 2 * NP,), jnp.int32),
            pltpu.SMEM((1,), jnp.int32),
            pltpu.VMEM(jac.shape, BF16),
            pltpu.VMEM(desc.shape, BF16),
            pltpu.VMEM((PCOLS, PCOLS) if fast else (TR, TL), BF16),
            pltpu.VMEM((2, 2, PB, TL), F32),
            pltpu.VMEM((NP, TR, TL), F32),
            pltpu.VMEM((NP, TR, TL), BF16),
            pltpu.VMEM((NP, TR, TL), BF16),
            pltpu.VMEM((total, NP * TR), BF16),
            pltpu.VMEM((total, TL), BF16),
            pltpu.VMEM((NZ, total, TL), BF16),
            pltpu.VMEM((3 * SLOTS, NZ * total), BF16),
            pltpu.VMEM((3 * SLOTS, TL), BF16),
            dma((5,)), dma, dma, dma, dma, dma, dma((NCH - 1,)), dma, dma,
        ],
        compiler_params=pltpu.CompilerParams(
            collective_id=0 if fast else 1, has_side_effects=True, vmem_limit_bytes=24 * 2**20
        ),
    )(order, panel, jac, desc, inv)


def run_compute(own, everything, inv, perm):
    rows = 2 * NC
    return pl.pallas_call(
        compute,
        name="compute",
        out_shape=(jax.ShapeDtypeStruct((rows, PCOLS), BF16),) * 2,
        in_specs=[VM] * 4,
        out_specs=(VM, VM),
        scratch_shapes=[
            pltpu.VMEM((2, PCOLS, 2 * TL), BF16),
            pltpu.VMEM((PCOLS + TR, 2 * TL), BF16),
            pltpu.VMEM((PCOLS, 2 * TL), BF16),
            pltpu.VMEM((2 * TL, 2 * TL), BF16),
            pltpu.VMEM((PCOLS, PCOLS), BF16),
            pltpu.VMEM((rows, PCOLS), F32),
        ],
        compiler_params=pltpu.CompilerParams(vmem_limit_bytes=40 * 2**20),
    )(own, everything, inv, perm)


def shards(jacobians, descriptors, block_inverse, tile_order, panel):
    jac = jnp.transpose(jacobians, (1, 0, 2))
    args = (tile_order, panel, jac, descriptors, block_inverse)
    own, few, inv, perm, over = run_exchange(True, *args)

    outs = run_compute(own, few, inv, perm)

    def usual(outs):
        return outs

    def crowded(outs):
        again, everything = run_exchange(False, *args)
        return run_compute(again, everything, inv, perm)

    return lax.cond(over[0] == 0, usual, crowded, outs)


def solution(mesh):
    placed = (P(("row", "col"), None, None), P(("row", "col"), None), P(), P(), P())
    return jax.shard_map(
        shards,
        mesh=mesh,
        in_specs=placed,
        out_specs=(P(("row", "col"), None), P(("row", "col"), None)),
        check_vma=False,
    )
```

```python
import functools
import math

import jax
import jax.numpy as jnp
from jax import lax
from jax.experimental import pallas as pl
from jax.experimental.pallas import tpu as pltpu
from jax.sharding import PartitionSpec as P

MESH = pl.DeviceIdType.MESH
F32 = jnp.float32
BF16 = jnp.bfloat16
NC = 60
ND = 190
PB = 64
TR = 16
TL = 128
PR = 8
NZ = 16
NCH = 16
NP = 32
SLOTS = 32
PCOLS = 960

NT = (((1,), (1,)), ((), ()))
NN = (((1,), (0,)), ((), ()))


def dot(a, b, dims):
    return lax.dot_general(a, b, dims, preferred_element_type=F32)


def iota(shape, dim):
    return lax.broadcasted_iota(jnp.int32, shape, dim)


def onehot(cond):
    return jnp.where(cond, 1.0, 0.0).astype(BF16)


def own_blocks(jac, desc_ref, blk, stage, send1, own_ref):
    lane = iota((1, TL), 1)
    low = lane < 64
    sums = jnp.logical_and(lane % 64 >= 62, lane >= 0)
    blk[...] = jnp.zeros_like(blk)
    stage[...] = jnp.zeros_like(stage)
    jac32 = jac[...].astype(F32)
    for i in range(2):
        one = jac32[:, i, :]
        desc32 = desc_ref[i : i + 1, :].astype(F32)
        col = jnp.sum(one * desc32, axis=1, keepdims=True)
        high = col.astype(BF16).astype(F32)
        blk[i, 0, 0:NC, :] = one[:, 0:TL]
        blk[i, 0, NC : NC + 1, :] = desc32[:, 0:TL]
        blk[i, 1, 0:NC, 0 : ND - TL] = one[:, TL:ND]
        blk[i, 1, 0:NC, ND - TL : ND - TL + 1] = high
        blk[i, 1, 0:NC, ND - TL + 1 : ND - TL + 2] = col - high
        blk[i, 1, NC : NC + 1, 0 : ND - TL] = desc32[:, TL:ND]
        rest = blk[i, 1]
        both = rest + pltpu.roll(rest, 64, 1)
        is_desc = iota((PB, TL), 0) == NC
        rows = slice(PB * i, PB * i + PB)
        own_ref[rows, 0:TL] = blk[i, 0].astype(BF16)
        own_ref[rows, TL : 2 * TL] = jnp.where(sums, jnp.where(is_desc, -1.0, 0.0), both).astype(BF16)
        own_ref[rows, 2 * TL : 3 * TL] = rest.astype(BF16)
        even = blk[i, 1, pl.ds(0, NP, stride=2), :]
        odd = blk[i, 1, pl.ds(1, NP, stride=2), :]
        pair = jnp.where(low, even, pltpu.roll(odd, 64, 1))
        for q in range(NP):
            stage[q, 2 * i : 2 * i + 2, :] = blk[i, 0, 2 * q : 2 * q + 2, :]
            stage[q, 4 + i : 5 + i, :] = pair[q : q + 1, :]
    for q in range(NP):
        send1[q] = stage[q].astype(BF16)


def choices(order, panel, z, cap, step, total, one1, one2, over_ref, fast):
    base = panel[0] * TR
    lane = iota((8, TL), 1)
    sub = iota((8, TL), 0)
    parts = []
    line = jnp.zeros((8, TL), jnp.int32)
    for g in range(SLOTS // 8):
        part = jnp.zeros((8, TL), jnp.int32)
        for s in range(8 * g, 8 * g + 8):
            conf = order[base + s]
            part = jnp.where(sub == s - 8 * g, conf, part)
            line = jnp.where(lane == s, conf, line)
        parts.append(part)
    conf_col = jnp.concatenate(parts, axis=0)
    conf_row = jnp.concatenate([line] * 4, axis=0)
    plane_col = conf_col // (2 * NP)
    plane_row = conf_row // (2 * NP)
    slot_col = iota((SLOTS, TL), 0)
    slot_row = iota((SLOTS, TL), 1)
    same = plane_col == plane_row
    before = jnp.logical_and(same, slot_row < slot_col)
    rank_col = jnp.sum(jnp.where(before, 1.0, 0.0), axis=1, keepdims=True)
    if over_ref is not None:
        over_ref[0] = jnp.where(jnp.max(rank_col) >= cap, 1, 0)
    rank_col = jnp.broadcast_to(rank_col, (SLOTS, TL)).astype(jnp.int32)
    place = rank_col if fast else slot_col
    here = plane_col == z
    device = (conf_col // 2) % NP
    which = conf_col % 2
    finds = []
    for kind in range(3):
        at = device * PR + (2 * which + kind if kind < 2 else 4 + which)
        find = []
        for t in range(NP * PR // TL):
            find.append(jnp.logical_and(at == slot_row + TL * t, here))
        finds.append(onehot(jnp.concatenate(find, axis=1)))
        goal = plane_col * total + kind * step + place
        take = [goal == slot_row + TL * t for t in range(NZ * total // TL)]
        one2[kind * SLOTS : kind * SLOTS + SLOTS, :] = onehot(jnp.concatenate(take, axis=1))
    finds = jnp.concatenate(finds, axis=0)
    if fast:
        after = jnp.logical_and(same, slot_col < slot_row)
        rank_row = jnp.sum(jnp.where(after, 1.0, 0.0), axis=0, keepdims=True).astype(jnp.int32)
        row = iota((one1.shape[0], SLOTS), 0)
        packs = []
        for kind in range(3):
            here_row = plane_row[0:1, 0:SLOTS] == z
            hit = jnp.logical_and(row == kind * step + rank_row[:, 0:SLOTS], rank_row[:, 0:SLOTS] < cap)
            packs.append(jnp.where(jnp.logical_and(hit, here_row), 1.0, 0.0))
        pack = jnp.concatenate(packs, axis=1).astype(BF16)
        one1[...] = dot(pack, finds, NN).astype(BF16)
    else:
        one1[...] = finds


def exchange(cap, step, total, fast, *refs):
    order_ref, panel_ref, jac_ref, desc_ref, inv_ref = refs[:5]
    if fast:
        own_ref, all_ref, inv_out, perm_out, over_ref = refs[5:10]
        rest = refs[10:]
    else:
        own_ref, all_ref = refs[5:7]
        inv_out = perm_out = over_ref = None
        rest = refs[7:]
    (order, panel, jac, desc, inv, blk, stage, send1, got1, one1, send2, got2, one2, mine, ins,
     s1, r1, s2, r2, s4, r4, s5, r5) = rest
    z = lax.axis_index("row")
    col = lax.axis_index("col")
    core = col % 2
    chip = col // 2
    sib = chip * 2 + 1 - core

    barrier = pltpu.get_barrier_semaphore()
    far = sorted(range(1, NZ), key=lambda d: -min(d, NZ - d))
    for d in far:
        pl.semaphore_signal(barrier, inc=1, device_id=((z + d) % NZ, col), device_id_type=MESH)
    for d in range(1, NP):
        pl.semaphore_signal(barrier, inc=1, device_id=(z, (col + d) % NP), device_id_type=MESH)
    loads = [(jac_ref, jac), (desc_ref, desc), (order_ref, order), (panel_ref, panel)]
    if fast:
        loads.append((inv_ref, inv))
    loads = [pltpu.make_async_copy(a, b, ins.at[n]) for n, (a, b) in enumerate(loads)]
    for load in loads:
        load.start()
    loads[0].wait()
    loads[1].wait()
    own_blocks(jac, desc, blk, stage, send1, own_ref)
    pl.semaphore_wait(barrier, NZ - 1 + NP - 1)

    x, y = chip // 4, chip % 4
    steps = [(dx, dy) for dx in range(4) for dy in range(4)]
    steps.sort(key=lambda d: min(d[0], 4 - d[0]) + min(d[1], 4 - d[1]), reverse=True)
    for dx, dy, dc in [(dx, dy, dc) for dx, dy in steps for dc in range(2)]:
        if not (dx or dy or dc):
            continue
        to = (((x + dx) % 4) * 4 + (y + dy) % 4) * 2 + (core + dc) % 2
        pltpu.make_async_remote_copy(
            send1.at[to], got1.at[col], s1, r1, device_id=(z, to), device_id_type=MESH
        ).start()
    got1[col] = send1[col]
    loads[2].wait()
    loads[3].wait()
    choices(order, panel, z, cap, step, total, one1, one2, over_ref, fast)
    if fast:
        at = iota((PCOLS, PCOLS), 1)
        perm_out[...] = onehot(iota((PCOLS, PCOLS), 0) == (at % TR) * NC + at // TR)
        loads[4].wait()
    pltpu.make_async_copy(got1.at[0 : NP - 1], got1.at[0 : NP - 1], r1).wait()

    held = got1[...].astype(F32).reshape(NP * PR, TL).astype(BF16)
    send2[...] = dot(one1[...], held, NN)[0:total, :].astype(BF16)
    for d in far:
        pltpu.make_async_remote_copy(
            send2, got2.at[z], s2, r2, device_id=((z + d) % NZ, col), device_id_type=MESH
        ).start()
    got2[z] = send2[...]
    if fast:

        @pl.loop(0, 3)
        def _(g):
            rows = pl.ds(pl.multiple_of(g * 320, 320), 320)
            inv_out[rows, :] = dot(inv[rows, :], perm_out[...], NN).astype(BF16)

    pltpu.make_async_copy(got2.at[0 : NZ - 1], got2.at[0 : NZ - 1], r2).wait()
    held = got2[...].astype(F32).reshape(NZ * total, TL).astype(BF16)
    mine[...] = dot(one2[...], held, NN).astype(BF16)

    steps = steps[:-1]
    for n, (dx, dy) in enumerate(steps):
        to = (((x + dx) % 4) * 4 + (y + dy) % 4) * 2 + core
        pltpu.make_async_remote_copy(
            mine, all_ref.at[core, chip], s4, r4.at[n], device_id=(z, to), device_id_type=MESH
        ).start()
    pltpu.make_async_remote_copy(
        mine, all_ref.at[core, chip], s5, r5, device_id=(z, sib), device_id_type=MESH
    ).start()
    all_ref[core, chip] = mine[...]
    for n, (dx, dy) in reversed(list(enumerate(steps))):
        source = ((x + 4 - dx) % 4) * 4 + (y + 4 - dy) % 4
        landed = all_ref.at[core, source]
        pltpu.make_async_copy(landed, landed, r4.at[n]).wait()
        pltpu.make_async_remote_copy(
            landed, landed, s5, r5, device_id=(z, sib), device_id_type=MESH
        ).start()
    other = all_ref.at[1 - core]
    pltpu.make_async_copy(other, other, r5).wait()

    pltpu.make_async_copy(got1.at[0 : NP - 1], got1.at[0 : NP - 1], s1).wait()
    pltpu.make_async_copy(got2.at[0 : NZ - 1], got2.at[0 : NZ - 1], s2).wait()
    pltpu.make_async_copy(all_ref.at[0, 0:15], all_ref.at[0, 0:15], s4).wait()
    pltpu.make_async_copy(other, other, s5).wait()


def compute(own_ref, all_ref, inv_ref, perm_ref, factor_ref, next_ref, rhs, lhs, lhs2, dexp, cross, outs):
    width = 2.0 * math.sqrt(2.0 * ND)
    lane = iota((TR, TL), 1)
    low = lane < 64
    sums = lane % 64 >= 62
    last = jnp.logical_and(lane >= 62, low)

    def piece(row, kind, half):
        p = row // 2
        first = (kind * 2 + half) * TR
        return all_ref[p % 2, p // 2, first : first + TR, :]

    ds = []
    for half in range(2):
        for p in range(NC // 2 + 1):
            rest = piece(2 * p, 2, half).astype(F32)
            turned = pltpu.roll(rest, 64, 1)
            for odd in range(2):
                row = 2 * p + odd
                if row > NC:
                    continue
                xt = piece(row, odd, half)
                rows = slice(TR * row, TR * row + TR)
                mine = turned if odd else rest
                if row < NC:
                    rhs[half, rows, 0:TL] = xt
                    rhs[half, rows, TL : 2 * TL] = jnp.where(low != (odd == 1), rest, 0.0).astype(BF16)
                if half == 0:
                    both = jnp.where(low != (odd == 1), rest, turned)
                    lhs[rows, 0:TL] = xt
                    lhs[rows, TL : 2 * TL] = jnp.where(sums, -1.0 if row == NC else 0.0, both).astype(BF16)
                    if row < NC:
                        lhs2[rows, 0:TL] = xt
                        lhs2[rows, TL : 2 * TL] = mine.astype(BF16)
                if row == NC:
                    d0, d1 = xt.astype(F32), jnp.where(low, rest, 0.0)
                    ds.append((d0, d1))
                    e1 = jnp.where(last, -1.0, d1).astype(BF16)
                    for t in range(TL // TR):
                        to = slice(TL * half + TR * t, TL * half + TR * t + TR)
                        dexp[to, 0:TL] = xt
                        dexp[to, TL : 2 * TL] = e1

    zero = jnp.zeros((6, TL), F32)
    own_d = [own_ref[PB * i + NC - 12 : PB * i + PB - 0, :].astype(F32)[12:13] for i in range(2)]
    d0s = jnp.concatenate([ds[0][0]] + [d[:, 0:TL] for d in own_d] + [zero], axis=0)
    d1s = jnp.concatenate([ds[0][1]] + [jnp.where(low[0:1], d[:, 2 * TL :], 0.0) for d in own_d] + [zero], axis=0)
    f1s, f2s = [], []
    lane24 = iota((24, TL), 1) % TR
    for half in range(2):
        dist = jnp.zeros((24, TL), F32)
        for b in range(TR):
            u0 = d0s - ds[half][0][b : b + 1, :]
            u1 = d1s - ds[half][1][b : b + 1, :]
            dist = jnp.where(lane24 == b, jnp.sum(u0 * u0 + u1 * u1, axis=1, keepdims=True), dist)
        scaled = (math.sqrt(5.0) / width) * jnp.sqrt(dist)
        decay = jnp.exp(-scaled)
        f1s.append(decay * (1.0 + scaled))
        f2s.append(decay * (5.0 / (width * width)))

    def wide(tile):
        return jnp.concatenate([tile] * 8, axis=1)[:, 0:PCOLS]

    own_lhs = own_ref[:, 0 : 2 * TL]
    own_lhs2 = jnp.concatenate([own_ref[:, 0:TL], own_ref[:, 2 * TL :]], axis=1)
    prod2 = dot(own_lhs2, dexp[...], NT)
    tiles = []
    for half in range(2):
        prod = dot(own_lhs, rhs[half], NT)
        parts = []
        for i in range(2):
            rows = slice(PB * i, PB * i + PB)
            f1 = wide(f1s[half][TR + i : TR + i + 1, :])
            qq = wide(f2s[half][TR + i : TR + i + 1, :]) * prod[PB * i + NC : PB * i + NC + 1, :]
            p = wide(prod2[rows, TL * half : TL * half + TL])
            parts.append(prod[rows, :] * f1 + p * qq)
        tiles.append(jnp.concatenate(parts, axis=0))
    factor = dot(tiles[0].astype(BF16), inv_ref[...], NT)
    outs[0:NC, :] = factor[0:NC, :]
    outs[NC : 2 * NC, :] = factor[PB : PB + NC, :]
    factor_ref[...] = outs[...].astype(BF16)
    most = jnp.max(jnp.abs(factor), axis=1, keepdims=True)
    scale = jnp.ones_like(most)
    back = jnp.ones_like(most)
    for _ in range(4):
        large = most * scale > 2.0**24
        scale = jnp.where(large, scale * 2.0**-24, scale)
        back = jnp.where(large, back * 2.0**24, back)
    scaled_factor = (factor.astype(BF16).astype(F32) * scale).astype(BF16)

    qq = wide(f2s[1][0:TR, :]) * dot(lhs[PCOLS : PCOLS + TR, :], rhs[1], NT)
    f1 = wide(f1s[1][0:TR, :])

    for g in range(4):
        rows = slice(240 * g, 240 * g + 240)
        a = dot(lhs[rows, :], rhs[1], NT)
        b = dot(lhs2[rows, :], dexp[TL : 2 * TL, :], NT)
        got = []
        for n in range(15):
            part = slice(TR * n, TR * n + TR)
            got.append((a[part, :] * f1 + wide(b[part, :]) * qq).astype(BF16))
        cross[rows, :] = jnp.concatenate(got, axis=0)

    middle = dot(scaled_factor, inv_ref[...], NN)
    high = middle.astype(BF16)
    both = jnp.concatenate([high, (middle - high.astype(F32)).astype(BF16)], axis=0)
    change = dot(both, cross[...], NN)
    change = (change[0:TL, :] + change[TL : 2 * TL, :]) * back
    updated = (tiles[1] - change).astype(BF16)
    final = dot(updated, perm_ref[...], NT)
    outs[0:NC, :] = final[0:NC, :]
    outs[NC : 2 * NC, :] = final[PB : PB + NC, :]
    next_ref[...] = outs[...].astype(BF16)


VM = pl.BlockSpec(memory_space=pltpu.VMEM)
HBM = pl.BlockSpec(memory_space=pltpu.HBM)


def run_exchange(fast, order, panel, jac, desc, inv):
    cap, step, total = (8, 8, 24) if fast else (32, 32, 96)
    square = jax.ShapeDtypeStruct((PCOLS, PCOLS), BF16)
    outs = (
        jax.ShapeDtypeStruct((2 * PB, 3 * TL), BF16),
        jax.ShapeDtypeStruct((2, NCH, 3 * SLOTS, TL), BF16),
    )
    specs = (VM, VM)
    if fast:
        outs += (square, square, jax.ShapeDtypeStruct((1,), jnp.int32))
        specs += (VM, VM, pl.BlockSpec(memory_space=pltpu.SMEM))
    dma = pltpu.SemaphoreType.DMA
    return pl.pallas_call(
        functools.partial(exchange, cap, step, total, fast),
        name="exchange" if fast else "exchange_full",
        out_shape=outs,
        in_specs=[HBM] * 5,
        out_specs=specs,
        scratch_shapes=[
            pltpu.SMEM((NZ * 2 * NP,), jnp.int32),
            pltpu.SMEM((1,), jnp.int32),
            pltpu.VMEM(jac.shape, BF16),
            pltpu.VMEM(desc.shape, BF16),
            pltpu.VMEM((PCOLS, PCOLS) if fast else (TR, TL), BF16),
            pltpu.VMEM((2, 2, PB, TL), F32),
            pltpu.VMEM((NP, PR, TL), F32),
            pltpu.VMEM((NP, PR, TL), BF16),
            pltpu.VMEM((NP, PR, TL), BF16),
            pltpu.VMEM((-(-total // TR) * TR, NP * PR), BF16),
            pltpu.VMEM((total, TL), BF16),
            pltpu.VMEM((NZ, total, TL), BF16),
            pltpu.VMEM((3 * SLOTS, NZ * total), BF16),
            pltpu.VMEM((3 * SLOTS, TL), BF16),
            dma((5,)), dma, dma, dma, dma, dma, dma((NCH - 1,)), dma, dma,
        ],
        compiler_params=pltpu.CompilerParams(
            collective_id=0 if fast else 1, has_side_effects=True, vmem_limit_bytes=24 * 2**20
        ),
    )(order, panel, jac, desc, inv)


def run_compute(own, everything, inv, perm):
    rows = 2 * NC
    return pl.pallas_call(
        compute,
        name="compute",
        out_shape=(jax.ShapeDtypeStruct((rows, PCOLS), BF16),) * 2,
        in_specs=[VM] * 4,
        out_specs=(VM, VM),
        scratch_shapes=[
            pltpu.VMEM((2, PCOLS, 2 * TL), BF16),
            pltpu.VMEM((PCOLS + TR, 2 * TL), BF16),
            pltpu.VMEM((PCOLS, 2 * TL), BF16),
            pltpu.VMEM((2 * TL, 2 * TL), BF16),
            pltpu.VMEM((PCOLS, PCOLS), BF16),
            pltpu.VMEM((rows, PCOLS), F32),
        ],
        compiler_params=pltpu.CompilerParams(vmem_limit_bytes=40 * 2**20),
    )(own, everything, inv, perm)


def shards(jacobians, descriptors, block_inverse, tile_order, panel):
    jac = jnp.transpose(jacobians, (1, 0, 2))
    args = (tile_order, panel, jac, descriptors, block_inverse)
    own, few, inv, perm, over = run_exchange(True, *args)

    outs = run_compute(own, few, inv, perm)

    def usual(outs):
        return outs

    def crowded(outs):
        again, everything = run_exchange(False, *args)
        return run_compute(again, everything, inv, perm)

    return lax.cond(over[0] == 0, usual, crowded, outs)


def solution(mesh):
    placed = (P(("row", "col"), None, None), P(("row", "col"), None), P(), P(), P())
    return jax.shard_map(
        shards,
        mesh=mesh,
        in_specs=placed,
        out_specs=(P(("row", "col"), None), P(("row", "col"), None)),
        check_vma=False,
    )
```

```python
import functools
import math

import jax
import jax.numpy as jnp
from jax import lax
from jax.experimental import pallas as pl
from jax.experimental.pallas import tpu as pltpu
from jax.sharding import PartitionSpec as P

MESH = pl.DeviceIdType.MESH
F32 = jnp.float32
BF16 = jnp.bfloat16
NC = 60
ND = 190
PB = 64
TR = 16
TL = 128
PR = 8
NZ = 16
NCH = 16
NP = 32
SLOTS = 32
PCOLS = 960

NT = (((1,), (1,)), ((), ()))
NN = (((1,), (0,)), ((), ()))


def dot(a, b, dims):
    return lax.dot_general(a, b, dims, preferred_element_type=F32)


def iota(shape, dim):
    return lax.broadcasted_iota(jnp.int32, shape, dim)


def onehot(cond):
    return jnp.where(cond, 1.0, 0.0).astype(BF16)


def own_blocks(jac, desc_ref, blk, stage, send1, own_ref):
    lane = iota((1, TL), 1)
    low = lane < 64
    sums = jnp.logical_and(lane % 64 >= 62, lane >= 0)
    blk[...] = jnp.zeros_like(blk)
    stage[...] = jnp.zeros_like(stage)
    jac32 = jac[...].astype(F32)
    for i in range(2):
        one = jac32[:, i, :]
        desc32 = desc_ref[i : i + 1, :].astype(F32)
        col = jnp.sum(one * desc32, axis=1, keepdims=True)
        high = col.astype(BF16).astype(F32)
        blk[i, 0, 0:NC, :] = one[:, 0:TL]
        blk[i, 0, NC : NC + 1, :] = desc32[:, 0:TL]
        blk[i, 1, 0:NC, 0 : ND - TL] = one[:, TL:ND]
        blk[i, 1, 0:NC, ND - TL : ND - TL + 1] = high
        blk[i, 1, 0:NC, ND - TL + 1 : ND - TL + 2] = col - high
        blk[i, 1, NC : NC + 1, 0 : ND - TL] = desc32[:, TL:ND]
        rest = blk[i, 1]
        both = rest + pltpu.roll(rest, 64, 1)
        is_desc = iota((PB, TL), 0) == NC
        rows = slice(PB * i, PB * i + PB)
        own_ref[rows, 0:TL] = blk[i, 0].astype(BF16)
        own_ref[rows, TL : 2 * TL] = jnp.where(sums, jnp.where(is_desc, -1.0, 0.0), both).astype(BF16)
        own_ref[rows, 2 * TL : 3 * TL] = rest.astype(BF16)
        even = blk[i, 1, pl.ds(0, NP, stride=2), :]
        odd = blk[i, 1, pl.ds(1, NP, stride=2), :]
        pair = jnp.where(low, even, pltpu.roll(odd, 64, 1))
        for q in range(NP):
            stage[q, 2 * i : 2 * i + 2, :] = blk[i, 0, 2 * q : 2 * q + 2, :]
            stage[q, 4 + i : 5 + i, :] = pair[q : q + 1, :]
    for q in range(NP):
        send1[q] = stage[q].astype(BF16)


def choices(order, panel, z, cap, step, total, one1, one2, over_ref, fast):
    base = panel[0] * TR
    lane = iota((8, TL), 1)
    sub = iota((8, TL), 0)
    parts = []
    line = jnp.zeros((8, TL), jnp.int32)
    for g in range(SLOTS // 8):
        part = jnp.zeros((8, TL), jnp.int32)
        for s in range(8 * g, 8 * g + 8):
            conf = order[base + s]
            part = jnp.where(sub == s - 8 * g, conf, part)
            line = jnp.where(lane == s, conf, line)
        parts.append(part)
    conf_col = jnp.concatenate(parts, axis=0)
    conf_row = jnp.concatenate([line] * 4, axis=0)
    plane_col = conf_col // (2 * NP)
    plane_row = conf_row // (2 * NP)
    slot_col = iota((SLOTS, TL), 0)
    slot_row = iota((SLOTS, TL), 1)
    same = plane_col == plane_row
    before = jnp.logical_and(same, slot_row < slot_col)
    rank_col = jnp.sum(jnp.where(before, 1.0, 0.0), axis=1, keepdims=True)
    if over_ref is not None:
        over_ref[0] = jnp.where(jnp.max(rank_col) >= cap, 1, 0)
    rank_col = jnp.broadcast_to(rank_col, (SLOTS, TL)).astype(jnp.int32)
    place = rank_col if fast else slot_col
    here = plane_col == z
    device = (conf_col // 2) % NP
    which = conf_col % 2
    finds = []
    for kind in range(3):
        at = device * PR + (2 * which + kind if kind < 2 else 4 + which)
        find = []
        for t in range(NP * PR // TL):
            find.append(jnp.logical_and(at == slot_row + TL * t, here))
        finds.append(onehot(jnp.concatenate(find, axis=1)))
        goal = plane_col * total + kind * step + place
        take = [goal == slot_row + TL * t for t in range(NZ * total // TL)]
        one2[kind * SLOTS : kind * SLOTS + SLOTS, :] = onehot(jnp.concatenate(take, axis=1))
    finds = jnp.concatenate(finds, axis=0)
    if fast:
        after = jnp.logical_and(same, slot_col < slot_row)
        rank_row = jnp.sum(jnp.where(after, 1.0, 0.0), axis=0, keepdims=True).astype(jnp.int32)
        row = iota((one1.shape[0], SLOTS), 0)
        packs = []
        for kind in range(3):
            here_row = plane_row[0:1, 0:SLOTS] == z
            hit = jnp.logical_and(row == kind * step + rank_row[:, 0:SLOTS], rank_row[:, 0:SLOTS] < cap)
            packs.append(jnp.where(jnp.logical_and(hit, here_row), 1.0, 0.0))
        pack = jnp.concatenate(packs, axis=1).astype(BF16)
        one1[...] = dot(pack, finds, NN).astype(BF16)
    else:
        one1[...] = finds


def exchange(cap, step, total, fast, *refs):
    order_ref, panel_ref, jac_ref, desc_ref, inv_ref = refs[:5]
    if fast:
        own_ref, all_ref, inv_out, perm_out, over_ref = refs[5:10]
        rest = refs[10:]
    else:
        own_ref, all_ref = refs[5:7]
        inv_out = perm_out = over_ref = None
        rest = refs[7:]
    (order, panel, jac, desc, inv, blk, stage, send1, got1, one1, send2, got2, one2, mine, ins,
     s1, r1, s2, r2, s4, r4, s5, r5, plane, line) = rest
    z = lax.axis_index("row")
    col = lax.axis_index("col")
    core = col % 2
    chip = col // 2
    sib = chip * 2 + 1 - core

    barrier = pltpu.get_barrier_semaphore()
    far = sorted(range(1, NZ), key=lambda d: -min(d, NZ - d))
    for d in far:
        pl.semaphore_signal(barrier, inc=1, device_id=((z + d) % NZ, 2 * chip + 1), device_id_type=MESH)
    for d in range(1, NCH):
        pl.semaphore_signal(barrier, inc=1, device_id=(z, (chip + d) % NCH * 2), device_id_type=MESH)

    @pl.when(core == 1)
    def _():
        pl.semaphore_signal(barrier, inc=1, device_id=(z, sib), device_id_type=MESH)

    loads = [(jac_ref, jac), (desc_ref, desc), (order_ref, order), (panel_ref, panel)]
    if fast:
        loads.append((inv_ref, inv))
    loads = [pltpu.make_async_copy(a, b, ins.at[n]) for n, (a, b) in enumerate(loads)]
    for load in loads:
        load.start()
    loads[0].wait()
    loads[1].wait()
    own_blocks(jac, desc, blk, stage, send1, own_ref)

    @pl.when(core == 0)
    def _():
        pl.semaphore_wait(barrier, NP - 1)
        pl.semaphore_signal(plane, inc=1, device_id=(z, sib), device_id_type=MESH)

    @pl.when(core == 1)
    def _():
        pl.semaphore_wait(plane, 1)

    x, y = chip // 4, chip % 4
    steps = [(dx, dy) for dx in range(4) for dy in range(4)]
    steps.sort(key=lambda d: min(d[0], 4 - d[0]) + min(d[1], 4 - d[1]), reverse=True)
    for dx, dy, dc in [(dx, dy, dc) for dx, dy in steps for dc in range(2)]:
        if not (dx or dy or dc):
            continue
        to = (((x + dx) % 4) * 4 + (y + dy) % 4) * 2 + (core + dc) % 2
        pltpu.make_async_remote_copy(
            send1.at[to], got1.at[col], s1, r1, device_id=(z, to), device_id_type=MESH
        ).start()
    got1[col] = send1[col]
    loads[2].wait()
    loads[3].wait()
    choices(order, panel, z, cap, step, total, one1, one2, over_ref, fast)
    if fast:
        at = iota((PCOLS, PCOLS), 1)
        perm_out[...] = onehot(iota((PCOLS, PCOLS), 0) == (at % TR) * NC + at // TR)
        loads[4].wait()

    @pl.when(core == 1)
    def _():
        pl.semaphore_wait(barrier, 2 * (NZ - 1))
        pl.semaphore_signal(line, inc=1, device_id=(z, sib), device_id_type=MESH)

    @pl.when(core == 0)
    def _():
        pl.semaphore_wait(line, 1)

    pltpu.make_async_copy(got1.at[0 : NP - 1], got1.at[0 : NP - 1], r1).wait()

    held = got1[...].astype(F32).reshape(NP * PR, TL).astype(BF16)
    send2[...] = dot(one1[...], held, NN)[0:total, :].reshape(total // PR, PR, TL).astype(BF16)
    for d in far:
        pltpu.make_async_remote_copy(
            send2, got2.at[z], s2, r2, device_id=((z + d) % NZ, col), device_id_type=MESH
        ).start()
    got2[z] = send2[...]
    if fast:

        @pl.loop(0, 3)
        def _(g):
            rows = pl.ds(pl.multiple_of(g * 320, 320), 320)
            inv_out[rows, :] = dot(inv[rows, :], perm_out[...], NN).astype(BF16)

    pltpu.make_async_copy(got2.at[0 : NZ - 1], got2.at[0 : NZ - 1], r2).wait()
    held = got2[...].astype(F32).reshape(NZ * total, TL).astype(BF16)
    mine[...] = dot(one2[...], held, NN).astype(BF16)

    steps = steps[:-1]
    for n, (dx, dy) in enumerate(steps):
        to = (((x + dx) % 4) * 4 + (y + dy) % 4) * 2 + core
        pltpu.make_async_remote_copy(
            mine, all_ref.at[core, chip], s4, r4.at[n], device_id=(z, to), device_id_type=MESH
        ).start()
    pltpu.make_async_remote_copy(
        mine, all_ref.at[core, chip], s5, r5, device_id=(z, sib), device_id_type=MESH
    ).start()
    all_ref[core, chip] = mine[...]
    for n, (dx, dy) in reversed(list(enumerate(steps))):
        source = ((x + 4 - dx) % 4) * 4 + (y + 4 - dy) % 4
        landed = all_ref.at[core, source]
        pltpu.make_async_copy(landed, landed, r4.at[n]).wait()
        pltpu.make_async_remote_copy(
            landed, landed, s5, r5, device_id=(z, sib), device_id_type=MESH
        ).start()
    other = all_ref.at[1 - core]
    pltpu.make_async_copy(other, other, r5).wait()

    pltpu.make_async_copy(got1.at[0 : NP - 1], got1.at[0 : NP - 1], s1).wait()
    pltpu.make_async_copy(got2.at[0 : NZ - 1], got2.at[0 : NZ - 1], s2).wait()
    pltpu.make_async_copy(all_ref.at[0, 0:15], all_ref.at[0, 0:15], s4).wait()
    pltpu.make_async_copy(other, other, s5).wait()


def compute(own_ref, all_ref, inv_ref, perm_ref, factor_ref, next_ref, rhs, lhs, lhs2, dexp, cross, outs):
    width = 2.0 * math.sqrt(2.0 * ND)
    lane = iota((TR, TL), 1)
    low = lane < 64
    sums = lane % 64 >= 62
    last = jnp.logical_and(lane >= 62, low)

    def piece(row, kind, half):
        p = row // 2
        first = (kind * 2 + half) * TR
        return all_ref[p % 2, p // 2, first : first + TR, :]

    ds = []
    for half in range(2):
        for p in range(NC // 2 + 1):
            rest = piece(2 * p, 2, half).astype(F32)
            turned = pltpu.roll(rest, 64, 1)
            for odd in range(2):
                row = 2 * p + odd
                if row > NC:
                    continue
                xt = piece(row, odd, half)
                rows = slice(TR * row, TR * row + TR)
                mine = turned if odd else rest
                if row < NC:
                    rhs[half, rows, 0:TL] = xt
                    rhs[half, rows, TL : 2 * TL] = jnp.where(low != (odd == 1), rest, 0.0).astype(BF16)
                if half == 0:
                    both = jnp.where(low != (odd == 1), rest, turned)
                    lhs[rows, 0:TL] = xt
                    lhs[rows, TL : 2 * TL] = jnp.where(sums, -1.0 if row == NC else 0.0, both).astype(BF16)
                    if row < NC:
                        lhs2[rows, 0:TL] = xt
                        lhs2[rows, TL : 2 * TL] = mine.astype(BF16)
                if row == NC:
                    d0, d1 = xt.astype(F32), jnp.where(low, rest, 0.0)
                    ds.append((d0, d1))
                    e1 = jnp.where(last, -1.0, d1).astype(BF16)
                    for t in range(TL // TR):
                        to = slice(TL * half + TR * t, TL * half + TR * t + TR)
                        dexp[to, 0:TL] = xt
                        dexp[to, TL : 2 * TL] = e1

    zero = jnp.zeros((6, TL), F32)
    own_d = [own_ref[PB * i + NC - 12 : PB * i + PB - 0, :].astype(F32)[12:13] for i in range(2)]
    d0s = jnp.concatenate([ds[0][0]] + [d[:, 0:TL] for d in own_d] + [zero], axis=0)
    d1s = jnp.concatenate([ds[0][1]] + [jnp.where(low[0:1], d[:, 2 * TL :], 0.0) for d in own_d] + [zero], axis=0)
    f1s, f2s = [], []
    lane24 = iota((24, TL), 1) % TR
    for half in range(2):
        dist = jnp.zeros((24, TL), F32)
        for b in range(TR):
            u0 = d0s - ds[half][0][b : b + 1, :]
            u1 = d1s - ds[half][1][b : b + 1, :]
            dist = jnp.where(lane24 == b, jnp.sum(u0 * u0 + u1 * u1, axis=1, keepdims=True), dist)
        scaled = (math.sqrt(5.0) / width) * jnp.sqrt(dist)
        decay = jnp.exp(-scaled)
        f1s.append(decay * (1.0 + scaled))
        f2s.append(decay * (5.0 / (width * width)))

    def wide(tile):
        return jnp.concatenate([tile] * 8, axis=1)[:, 0:PCOLS]

    own_lhs = own_ref[:, 0 : 2 * TL]
    own_lhs2 = jnp.concatenate([own_ref[:, 0:TL], own_ref[:, 2 * TL :]], axis=1)
    prod2 = dot(own_lhs2, dexp[...], NT)
    tiles = []
    for half in range(2):
        prod = dot(own_lhs, rhs[half], NT)
        parts = []
        for i in range(2):
            rows = slice(PB * i, PB * i + PB)
            f1 = wide(f1s[half][TR + i : TR + i + 1, :])
            qq = wide(f2s[half][TR + i : TR + i + 1, :]) * prod[PB * i + NC : PB * i + NC + 1, :]
            p = wide(prod2[rows, TL * half : TL * half + TL])
            parts.append(prod[rows, :] * f1 + p * qq)
        tiles.append(jnp.concatenate(parts, axis=0))
    factor = dot(tiles[0].astype(BF16), inv_ref[...], NT)
    outs[0:NC, :] = factor[0:NC, :]
    outs[NC : 2 * NC, :] = factor[PB : PB + NC, :]
    factor_ref[...] = outs[...].astype(BF16)
    most = jnp.max(jnp.abs(factor), axis=1, keepdims=True)
    scale = jnp.ones_like(most)
    back = jnp.ones_like(most)
    for _ in range(4):
        large = most * scale > 2.0**24
        scale = jnp.where(large, scale * 2.0**-24, scale)
        back = jnp.where(large, back * 2.0**24, back)
    scaled_factor = (factor.astype(BF16).astype(F32) * scale).astype(BF16)

    qq = wide(f2s[1][0:TR, :]) * dot(lhs[PCOLS : PCOLS + TR, :], rhs[1], NT)
    f1 = wide(f1s[1][0:TR, :])

    for g in range(4):
        rows = slice(240 * g, 240 * g + 240)
        a = dot(lhs[rows, :], rhs[1], NT)
        b = dot(lhs2[rows, :], dexp[TL : 2 * TL, :], NT)
        got = []
        for n in range(15):
            part = slice(TR * n, TR * n + TR)
            got.append((a[part, :] * f1 + wide(b[part, :]) * qq).astype(BF16))
        cross[rows, :] = jnp.concatenate(got, axis=0)

    middle = dot(scaled_factor, inv_ref[...], NN)
    high = middle.astype(BF16)
    both = jnp.concatenate([high, (middle - high.astype(F32)).astype(BF16)], axis=0)
    change = dot(both, cross[...], NN)
    change = (change[0:TL, :] + change[TL : 2 * TL, :]) * back
    updated = (tiles[1] - change).astype(BF16)
    final = dot(updated, perm_ref[...], NT)
    outs[0:NC, :] = final[0:NC, :]
    outs[NC : 2 * NC, :] = final[PB : PB + NC, :]
    next_ref[...] = outs[...].astype(BF16)


VM = pl.BlockSpec(memory_space=pltpu.VMEM)
HBM = pl.BlockSpec(memory_space=pltpu.HBM)


def run_exchange(fast, order, panel, jac, desc, inv):
    cap, step, total = (8, 8, 24) if fast else (32, 32, 96)
    square = jax.ShapeDtypeStruct((PCOLS, PCOLS), BF16)
    outs = (
        jax.ShapeDtypeStruct((2 * PB, 3 * TL), BF16),
        jax.ShapeDtypeStruct((2, NCH, 3 * SLOTS, TL), BF16),
    )
    specs = (VM, VM)
    if fast:
        outs += (square, square, jax.ShapeDtypeStruct((1,), jnp.int32))
        specs += (VM, VM, pl.BlockSpec(memory_space=pltpu.SMEM))
    dma = pltpu.SemaphoreType.DMA
    return pl.pallas_call(
        functools.partial(exchange, cap, step, total, fast),
        name="exchange" if fast else "exchange_full",
        out_shape=outs,
        in_specs=[HBM] * 5,
        out_specs=specs,
        scratch_shapes=[
            pltpu.SMEM((NZ * 2 * NP,), jnp.int32),
            pltpu.SMEM((1,), jnp.int32),
            pltpu.VMEM(jac.shape, BF16),
            pltpu.VMEM(desc.shape, BF16),
            pltpu.VMEM((PCOLS, PCOLS) if fast else (TR, TL), BF16),
            pltpu.VMEM((2, 2, PB, TL), F32),
            pltpu.VMEM((NP, PR, TL), F32),
            pltpu.VMEM((NP, PR, TL), BF16),
            pltpu.VMEM((NP, PR, TL), BF16),
            pltpu.VMEM((-(-total // TR) * TR, NP * PR), BF16),
            pltpu.VMEM((total // PR, PR, TL), BF16),
            pltpu.VMEM((NZ, total // PR, PR, TL), BF16),
            pltpu.VMEM((3 * SLOTS, NZ * total), BF16),
            pltpu.VMEM((3 * SLOTS, TL), BF16),
            dma((5,)), dma, dma, dma, dma, dma, dma((NCH - 1,)), dma, dma,
            pltpu.SemaphoreType.REGULAR, pltpu.SemaphoreType.REGULAR,
        ],
        compiler_params=pltpu.CompilerParams(
            collective_id=0 if fast else 1, has_side_effects=True, vmem_limit_bytes=24 * 2**20
        ),
    )(order, panel, jac, desc, inv)


def run_compute(own, everything, inv, perm):
    rows = 2 * NC
    return pl.pallas_call(
        compute,
        name="compute",
        out_shape=(jax.ShapeDtypeStruct((rows, PCOLS), BF16),) * 2,
        in_specs=[VM] * 4,
        out_specs=(VM, VM),
        scratch_shapes=[
            pltpu.VMEM((2, PCOLS, 2 * TL), BF16),
            pltpu.VMEM((PCOLS + TR, 2 * TL), BF16),
            pltpu.VMEM((PCOLS, 2 * TL), BF16),
            pltpu.VMEM((2 * TL, 2 * TL), BF16),
            pltpu.VMEM((PCOLS, PCOLS), BF16),
            pltpu.VMEM((rows, PCOLS), F32),
        ],
        compiler_params=pltpu.CompilerParams(vmem_limit_bytes=40 * 2**20),
    )(own, everything, inv, perm)


def shards(jacobians, descriptors, block_inverse, tile_order, panel):
    jac = jnp.transpose(jacobians, (1, 0, 2))
    args = (tile_order, panel, jac, descriptors, block_inverse)
    own, few, inv, perm, over = run_exchange(True, *args)

    outs = run_compute(own, few, inv, perm)

    def usual(outs):
        return outs

    def crowded(outs):
        again, everything = run_exchange(False, *args)
        return run_compute(again, everything, inv, perm)

    return lax.cond(over[0] == 0, usual, crowded, outs)


def solution(mesh):
    placed = (P(("row", "col"), None, None), P(("row", "col"), None), P(), P(), P())
    return jax.shard_map(
        shards,
        mesh=mesh,
        in_specs=placed,
        out_specs=(P(("row", "col"), None), P(("row", "col"), None)),
        check_vma=False,
    )
```

```python
import functools
import math

import jax
import jax.numpy as jnp
from jax import lax
from jax.experimental import pallas as pl
from jax.experimental.pallas import tpu as pltpu
from jax.sharding import PartitionSpec as P

MESH = pl.DeviceIdType.MESH
F32 = jnp.float32
BF16 = jnp.bfloat16
NC = 60
ND = 190
PB = 64
TR = 16
TL = 128
PR = 8
NZ = 16
NCH = 16
NP = 32
SLOTS = 32
PCOLS = 960

NT = (((1,), (1,)), ((), ()))
NN = (((1,), (0,)), ((), ()))


def dot(a, b, dims):
    return lax.dot_general(a, b, dims, preferred_element_type=F32)


def iota(shape, dim):
    return lax.broadcasted_iota(jnp.int32, shape, dim)


def onehot(cond):
    return jnp.where(cond, 1.0, 0.0).astype(BF16)


def own_blocks(jac, desc_ref, blk, stage, send1, own_ref):
    lane = iota((1, TL), 1)
    low = lane < 64
    sums = jnp.logical_and(lane % 64 >= 62, lane >= 0)
    blk[...] = jnp.zeros_like(blk)
    stage[...] = jnp.zeros_like(stage)
    jac32 = jac[...].astype(F32)
    for i in range(2):
        one = jac32[:, i, :]
        desc32 = desc_ref[i : i + 1, :].astype(F32)
        col = jnp.sum(one * desc32, axis=1, keepdims=True)
        high = col.astype(BF16).astype(F32)
        blk[i, 0, 0:NC, :] = one[:, 0:TL]
        blk[i, 0, NC : NC + 1, :] = desc32[:, 0:TL]
        blk[i, 1, 0:NC, 0 : ND - TL] = one[:, TL:ND]
        blk[i, 1, 0:NC, ND - TL : ND - TL + 1] = high
        blk[i, 1, 0:NC, ND - TL + 1 : ND - TL + 2] = col - high
        blk[i, 1, NC : NC + 1, 0 : ND - TL] = desc32[:, TL:ND]
        rest = blk[i, 1]
        both = rest + pltpu.roll(rest, 64, 1)
        is_desc = iota((PB, TL), 0) == NC
        rows = slice(PB * i, PB * i + PB)
        own_ref[rows, 0:TL] = blk[i, 0].astype(BF16)
        own_ref[rows, TL : 2 * TL] = jnp.where(sums, jnp.where(is_desc, -1.0, 0.0), both).astype(BF16)
        own_ref[rows, 2 * TL : 3 * TL] = rest.astype(BF16)
        even = blk[i, 1, pl.ds(0, NP, stride=2), :]
        odd = blk[i, 1, pl.ds(1, NP, stride=2), :]
        pair = jnp.where(low, even, pltpu.roll(odd, 64, 1))
        for q in range(NP):
            stage[q, 2 * i : 2 * i + 2, :] = blk[i, 0, 2 * q : 2 * q + 2, :]
            stage[q, 4 + i : 5 + i, :] = pair[q : q + 1, :]
    for q in range(NP):
        send1[q] = stage[q].astype(BF16)


def choices(order, panel, z, cap, step, one1, one2, flag, fast):
    base = panel[0] * TR
    lane = iota((8, TL), 1)
    sub = iota((8, TL), 0)
    parts = []
    line = jnp.zeros((8, TL), jnp.int32)
    for g in range(SLOTS // 8):
        part = jnp.zeros((8, TL), jnp.int32)
        for s in range(8 * g, 8 * g + 8):
            conf = order[base + s]
            part = jnp.where(sub == s - 8 * g, conf, part)
            line = jnp.where(lane == s, conf, line)
        parts.append(part)
    conf_col = jnp.concatenate(parts, axis=0)
    conf_row = jnp.concatenate([line] * 4, axis=0)
    plane_col = conf_col // (2 * NP)
    plane_row = conf_row // (2 * NP)
    slot_col = iota((SLOTS, TL), 0)
    slot_row = iota((SLOTS, TL), 1)
    same = plane_col == plane_row
    before = jnp.logical_and(same, slot_row < slot_col)
    rank_col = jnp.sum(jnp.where(before, 1.0, 0.0), axis=1, keepdims=True)
    if fast:
        flag[0] = jnp.where(jnp.max(rank_col) >= cap, 1, 0)
    rank_col = jnp.broadcast_to(rank_col, (SLOTS, TL)).astype(jnp.int32)
    place = rank_col if fast else slot_col
    here = plane_col == z
    device = (conf_col // 2) % NP
    which = conf_col % 2
    finds = []
    for kind in range(3):
        at = device * PR + (2 * which + kind if kind < 2 else 4 + which)
        find = []
        for t in range(NP * PR // TL):
            find.append(jnp.logical_and(at == slot_row + TL * t, here))
        finds.append(onehot(jnp.concatenate(find, axis=1)))
    goal = plane_col * step + place
    one2[...] = onehot(jnp.concatenate([goal == slot_row + TL * t for t in range(NZ * step // TL)], axis=1))
    finds = jnp.concatenate(finds, axis=0)
    if fast:
        after = jnp.logical_and(same, slot_col < slot_row)
        rank_row = jnp.sum(jnp.where(after, 1.0, 0.0), axis=0, keepdims=True).astype(jnp.int32)
        row = iota((one1.shape[0], SLOTS), 0)
        packs = []
        for kind in range(3):
            here_row = plane_row[0:1, 0:SLOTS] == z
            hit = jnp.logical_and(row == kind * step + rank_row[:, 0:SLOTS], rank_row[:, 0:SLOTS] < cap)
            packs.append(jnp.where(jnp.logical_and(hit, here_row), 1.0, 0.0))
        pack = jnp.concatenate(packs, axis=1).astype(BF16)
        one1[...] = dot(pack, finds, NN).astype(BF16)
    else:
        one1[...] = finds


def exchange(cap, step, total, fast, *refs):
    order_ref, panel_ref, jac_ref, desc_ref, inv_ref = refs[:5]
    if fast:
        own_ref, all_ref, inv_out, perm_out, over_ref = refs[5:10]
        rest = refs[10:]
    else:
        own_ref, all_ref = refs[5:7]
        inv_out = perm_out = over_ref = None
        rest = refs[7:]
    (flag, order, panel, jac, desc, inv, blk, stage, send1, got1, one1, send2, got2, one2, mine, ins,
     s1, r1, s2, r2, s4, r4, s5, r5, plane, line) = rest
    z = lax.axis_index("row")
    col = lax.axis_index("col")
    core = col % 2
    chip = col // 2
    sib = chip * 2 + 1 - core

    barrier = pltpu.get_barrier_semaphore()
    far = sorted(range(1, NZ), key=lambda d: -min(d, NZ - d))
    for d in far:
        pl.semaphore_signal(barrier, inc=1, device_id=((z + d) % NZ, 2 * chip + 1), device_id_type=MESH)
    for d in range(1, NCH):
        pl.semaphore_signal(barrier, inc=1, device_id=(z, (chip + d) % NCH * 2), device_id_type=MESH)

    @pl.when(core == 1)
    def _():
        pl.semaphore_signal(barrier, inc=1, device_id=(z, sib), device_id_type=MESH)

    loads = [(jac_ref, jac), (desc_ref, desc), (order_ref, order), (panel_ref, panel)]
    if fast:
        loads.append((inv_ref, inv))
    loads = [pltpu.make_async_copy(a, b, ins.at[n]) for n, (a, b) in enumerate(loads)]
    for load in loads:
        load.start()
    loads[0].wait()
    loads[1].wait()
    own_blocks(jac, desc, blk, stage, send1, own_ref)

    @pl.when(core == 0)
    def _():
        pl.semaphore_wait(barrier, NP - 1)
        pl.semaphore_signal(plane, inc=1, device_id=(z, sib), device_id_type=MESH)

    @pl.when(core == 1)
    def _():
        pl.semaphore_wait(plane, 1)

    x, y = chip // 4, chip % 4
    steps = [(dx, dy) for dx in range(4) for dy in range(4)]
    steps.sort(key=lambda d: min(d[0], 4 - d[0]) + min(d[1], 4 - d[1]), reverse=True)
    for dx, dy, dc in [(dx, dy, dc) for dx, dy in steps for dc in range(2)]:
        if not (dx or dy or dc):
            continue
        to = (((x + dx) % 4) * 4 + (y + dy) % 4) * 2 + (core + dc) % 2
        pltpu.make_async_remote_copy(
            send1.at[to], got1.at[col], s1, r1, device_id=(z, to), device_id_type=MESH
        ).start()
    got1[col] = send1[col]
    loads[2].wait()
    loads[3].wait()
    choices(order, panel, z, cap, step, one1, one2, flag, fast)
    if fast:
        told = pltpu.make_async_copy(flag, over_ref, ins.at[5])
        told.start()
        at = iota((PCOLS, PCOLS), 1)
        perm_out[...] = onehot(iota((PCOLS, PCOLS), 0) == (at % TR) * NC + at // TR)
        loads[4].wait()

    @pl.when(core == 1)
    def _():
        pl.semaphore_wait(barrier, 2 * (NZ - 1))
        pl.semaphore_signal(line, inc=1, device_id=(z, sib), device_id_type=MESH)

    @pl.when(core == 0)
    def _():
        pl.semaphore_wait(line, 1)

    pltpu.make_async_copy(got1.at[0 : NP - 1], got1.at[0 : NP - 1], r1).wait()

    held = got1[...].astype(F32).reshape(NP * PR, TL).astype(BF16)
    send2[...] = dot(one1[...], held, NN)[0:total, :].reshape(3, step // PR, PR, TL).astype(BF16)
    for kind in range(3):
        for d in far:
            pltpu.make_async_remote_copy(
                send2.at[kind], got2.at[kind, z], s2, r2.at[kind],
                device_id=((z + d) % NZ, col), device_id_type=MESH,
            ).start()
        got2[kind, z] = send2[kind]
    if fast:

        @pl.loop(0, 3)
        def _(g):
            rows = pl.ds(pl.multiple_of(g * 320, 320), 320)
            inv_out[rows, :] = dot(inv[rows, :], perm_out[...], NN).astype(BF16)

    steps = steps[:-1]
    for kind in range(3):
        part = got2.at[kind, 0 : NZ - 1]
        pltpu.make_async_copy(part, part, r2.at[kind]).wait()
        held = got2[kind].astype(F32).reshape(NZ * step, TL).astype(BF16)
        rows = pl.ds(kind * SLOTS, SLOTS)
        mine[rows, :] = dot(one2[...], held, NN).astype(BF16)
        for n, (dx, dy) in enumerate(steps):
            to = (((x + dx) % 4) * 4 + (y + dy) % 4) * 2 + core
            pltpu.make_async_remote_copy(
                mine.at[rows], all_ref.at[core, chip, rows], s4, r4.at[kind, n],
                device_id=(z, to), device_id_type=MESH,
            ).start()
        pltpu.make_async_remote_copy(
            mine.at[rows], all_ref.at[core, chip, rows], s5, r5, device_id=(z, sib), device_id_type=MESH
        ).start()
    all_ref[core, chip] = mine[...]
    for kind in range(3):
        rows = pl.ds(kind * SLOTS, SLOTS)
        for n, (dx, dy) in reversed(list(enumerate(steps))):
            source = ((x + 4 - dx) % 4) * 4 + (y + 4 - dy) % 4
            landed = all_ref.at[core, source, rows]
            pltpu.make_async_copy(landed, landed, r4.at[kind, n]).wait()
            pltpu.make_async_remote_copy(
                landed, landed, s5, r5, device_id=(z, sib), device_id_type=MESH
            ).start()
    other = all_ref.at[1 - core]
    pltpu.make_async_copy(other, other, r5).wait()

    pltpu.make_async_copy(got1.at[0 : NP - 1], got1.at[0 : NP - 1], s1).wait()
    every = got2.at[0:3, 0 : NZ - 1]
    pltpu.make_async_copy(every, every, s2).wait()
    pltpu.make_async_copy(all_ref.at[0, 0:15], all_ref.at[0, 0:15], s4).wait()
    pltpu.make_async_copy(other, other, s5).wait()
    if fast:
        told.wait()


def compute(own_ref, all_ref, inv_ref, perm_ref, factor_ref, next_ref, rhs, lhs, lhs2, dexp, cross, outs):
    width = 2.0 * math.sqrt(2.0 * ND)
    lane = iota((TR, TL), 1)
    low = lane < 64
    sums = lane % 64 >= 62
    last = jnp.logical_and(lane >= 62, low)

    def piece(row, kind, half):
        p = row // 2
        first = (kind * 2 + half) * TR
        return all_ref[p % 2, p // 2, first : first + TR, :]

    ds = []
    for half in range(2):
        for p in range(NC // 2 + 1):
            rest = piece(2 * p, 2, half).astype(F32)
            turned = pltpu.roll(rest, 64, 1)
            for odd in range(2):
                row = 2 * p + odd
                if row > NC:
                    continue
                xt = piece(row, odd, half)
                rows = slice(TR * row, TR * row + TR)
                mine = turned if odd else rest
                if row < NC:
                    rhs[half, rows, 0:TL] = xt
                    rhs[half, rows, TL : 2 * TL] = jnp.where(low != (odd == 1), rest, 0.0).astype(BF16)
                if half == 0:
                    both = jnp.where(low != (odd == 1), rest, turned)
                    lhs[rows, 0:TL] = xt
                    lhs[rows, TL : 2 * TL] = jnp.where(sums, -1.0 if row == NC else 0.0, both).astype(BF16)
                    if row < NC:
                        lhs2[rows, 0:TL] = xt
                        lhs2[rows, TL : 2 * TL] = mine.astype(BF16)
                if row == NC:
                    d0, d1 = xt.astype(F32), jnp.where(low, rest, 0.0)
                    ds.append((d0, d1))
                    e1 = jnp.where(last, -1.0, d1).astype(BF16)
                    for t in range(TL // TR):
                        to = slice(TL * half + TR * t, TL * half + TR * t + TR)
                        dexp[to, 0:TL] = xt
                        dexp[to, TL : 2 * TL] = e1

    zero = jnp.zeros((6, TL), F32)
    own_d = [own_ref[PB * i + NC - 12 : PB * i + PB - 0, :].astype(F32)[12:13] for i in range(2)]
    d0s = jnp.concatenate([ds[0][0]] + [d[:, 0:TL] for d in own_d] + [zero], axis=0)
    d1s = jnp.concatenate([ds[0][1]] + [jnp.where(low[0:1], d[:, 2 * TL :], 0.0) for d in own_d] + [zero], axis=0)
    f1s, f2s = [], []
    lane24 = iota((24, TL), 1) % TR
    for half in range(2):
        dist = jnp.zeros((24, TL), F32)
        for b in range(TR):
            u0 = d0s - ds[half][0][b : b + 1, :]
            u1 = d1s - ds[half][1][b : b + 1, :]
            dist = jnp.where(lane24 == b, jnp.sum(u0 * u0 + u1 * u1, axis=1, keepdims=True), dist)
        scaled = (math.sqrt(5.0) / width) * jnp.sqrt(dist)
        decay = jnp.exp(-scaled)
        f1s.append(decay * (1.0 + scaled))
        f2s.append(decay * (5.0 / (width * width)))

    def wide(tile):
        return jnp.concatenate([tile] * 8, axis=1)[:, 0:PCOLS]

    own_lhs = own_ref[:, 0 : 2 * TL]
    own_lhs2 = jnp.concatenate([own_ref[:, 0:TL], own_ref[:, 2 * TL :]], axis=1)
    prod2 = dot(own_lhs2, dexp[...], NT)
    tiles = []
    for half in range(2):
        prod = dot(own_lhs, rhs[half], NT)
        parts = []
        for i in range(2):
            rows = slice(PB * i, PB * i + PB)
            f1 = wide(f1s[half][TR + i : TR + i + 1, :])
            qq = wide(f2s[half][TR + i : TR + i + 1, :]) * prod[PB * i + NC : PB * i + NC + 1, :]
            p = wide(prod2[rows, TL * half : TL * half + TL])
            parts.append(prod[rows, :] * f1 + p * qq)
        tiles.append(jnp.concatenate(parts, axis=0))
    factor = dot(tiles[0].astype(BF16), inv_ref[...], NT)
    outs[0:NC, :] = factor[0:NC, :]
    outs[NC : 2 * NC, :] = factor[PB : PB + NC, :]
    factor_ref[...] = outs[...].astype(BF16)
    most = jnp.max(jnp.abs(factor), axis=1, keepdims=True)
    scale = jnp.ones_like(most)
    back = jnp.ones_like(most)
    for _ in range(4):
        large = most * scale > 2.0**24
        scale = jnp.where(large, scale * 2.0**-24, scale)
        back = jnp.where(large, back * 2.0**24, back)
    scaled_factor = (factor.astype(BF16).astype(F32) * scale).astype(BF16)

    qq = wide(f2s[1][0:TR, :]) * dot(lhs[PCOLS : PCOLS + TR, :], rhs[1], NT)
    f1 = wide(f1s[1][0:TR, :])

    for g in range(4):
        rows = slice(240 * g, 240 * g + 240)
        a = dot(lhs[rows, :], rhs[1], NT)
        b = dot(lhs2[rows, :], dexp[TL : 2 * TL, :], NT)
        got = []
        for n in range(15):
            part = slice(TR * n, TR * n + TR)
            got.append((a[part, :] * f1 + wide(b[part, :]) * qq).astype(BF16))
        cross[rows, :] = jnp.concatenate(got, axis=0)

    middle = dot(scaled_factor, inv_ref[...], NN)
    high = middle.astype(BF16)
    both = jnp.concatenate([high, (middle - high.astype(F32)).astype(BF16)], axis=0)
    change = dot(both, cross[...], NN)
    change = (change[0:TL, :] + change[TL : 2 * TL, :]) * back
    updated = (tiles[1] - change).astype(BF16)
    final = dot(updated, perm_ref[...], NT)
    outs[0:NC, :] = final[0:NC, :]
    outs[NC : 2 * NC, :] = final[PB : PB + NC, :]
    next_ref[...] = outs[...].astype(BF16)


VM = pl.BlockSpec(memory_space=pltpu.VMEM)
HBM = pl.BlockSpec(memory_space=pltpu.HBM)


def run_exchange(fast, order, panel, jac, desc, inv):
    cap, step, total = (8, 8, 24) if fast else (32, 32, 96)
    square = jax.ShapeDtypeStruct((PCOLS, PCOLS), BF16)
    outs = (
        jax.ShapeDtypeStruct((2 * PB, 3 * TL), BF16),
        jax.ShapeDtypeStruct((2, NCH, 3 * SLOTS, TL), BF16),
    )
    specs = (VM, VM)
    if fast:
        outs += (square, square, jax.ShapeDtypeStruct((1,), jnp.int32))
        specs += (VM, VM, HBM)
    dma = pltpu.SemaphoreType.DMA
    return pl.pallas_call(
        functools.partial(exchange, cap, step, total, fast),
        name="exchange" if fast else "exchange_full",
        out_shape=outs,
        in_specs=[HBM] * 5,
        out_specs=specs,
        scratch_shapes=[
            pltpu.SMEM((1,), jnp.int32),
            pltpu.SMEM((NZ * 2 * NP,), jnp.int32),
            pltpu.SMEM((1,), jnp.int32),
            pltpu.VMEM(jac.shape, BF16),
            pltpu.VMEM(desc.shape, BF16),
            pltpu.VMEM((PCOLS, PCOLS) if fast else (TR, TL), BF16),
            pltpu.VMEM((2, 2, PB, TL), F32),
            pltpu.VMEM((NP, PR, TL), F32),
            pltpu.VMEM((NP, PR, TL), BF16),
            pltpu.VMEM((NP, PR, TL), BF16),
            pltpu.VMEM((-(-total // TR) * TR, NP * PR), BF16),
            pltpu.VMEM((3, step // PR, PR, TL), BF16),
            pltpu.VMEM((3, NZ, step // PR, PR, TL), BF16),
            pltpu.VMEM((SLOTS, NZ * step), BF16),
            pltpu.VMEM((3 * SLOTS, TL), BF16),
            dma((6,)), dma, dma, dma, dma((3,)), dma, dma((3, NCH - 1)), dma, dma,
            pltpu.SemaphoreType.REGULAR, pltpu.SemaphoreType.REGULAR,
        ],
        compiler_params=pltpu.CompilerParams(
            collective_id=0 if fast else 1, has_side_effects=True, vmem_limit_bytes=24 * 2**20
        ),
    )(order, panel, jac, desc, inv)


def run_compute(own, everything, inv, perm):
    rows = 2 * NC
    return pl.pallas_call(
        compute,
        name="compute",
        out_shape=(jax.ShapeDtypeStruct((rows, PCOLS), BF16),) * 2,
        in_specs=[VM] * 4,
        out_specs=(VM, VM),
        scratch_shapes=[
            pltpu.VMEM((2, PCOLS, 2 * TL), BF16),
            pltpu.VMEM((PCOLS + TR, 2 * TL), BF16),
            pltpu.VMEM((PCOLS, 2 * TL), BF16),
            pltpu.VMEM((2 * TL, 2 * TL), BF16),
            pltpu.VMEM((PCOLS, PCOLS), BF16),
            pltpu.VMEM((rows, PCOLS), F32),
        ],
        compiler_params=pltpu.CompilerParams(vmem_limit_bytes=40 * 2**20),
    )(own, everything, inv, perm)


def shards(jacobians, descriptors, block_inverse, tile_order, panel):
    jac = jnp.transpose(jacobians, (1, 0, 2))
    args = (tile_order, panel, jac, descriptors, block_inverse)
    own, few, inv, perm, over = run_exchange(True, *args)

    outs = run_compute(own, few, inv, perm)

    def usual(outs):
        return outs

    def crowded(outs):
        again, everything = run_exchange(False, *args)
        return run_compute(again, everything, inv, perm)

    return lax.cond(over[0] == 0, usual, crowded, outs)


def solution(mesh):
    placed = (P(("row", "col"), None, None), P(("row", "col"), None), P(), P(), P())
    return jax.shard_map(
        shards,
        mesh=mesh,
        in_specs=placed,
        out_specs=(P(("row", "col"), None), P(("row", "col"), None)),
        check_vma=False,
    )
```

```python
import functools
import math

import jax
import jax.numpy as jnp
from jax import lax
from jax.experimental import pallas as pl
from jax.experimental.pallas import tpu as pltpu
from jax.sharding import PartitionSpec as P

MESH = pl.DeviceIdType.MESH
F32 = jnp.float32
BF16 = jnp.bfloat16
NC = 60
ND = 190
PB = 64
TR = 16
TL = 128
PR = 8
NZ = 16
NCH = 16
NP = 32
SLOTS = 32
PCOLS = 960

NT = (((1,), (1,)), ((), ()))
NN = (((1,), (0,)), ((), ()))


def dot(a, b, dims):
    return lax.dot_general(a, b, dims, preferred_element_type=F32)


def iota(shape, dim):
    return lax.broadcasted_iota(jnp.int32, shape, dim)


def onehot(cond):
    return jnp.where(cond, 1.0, 0.0).astype(BF16)


def own_blocks(jac, desc_ref, blk, stage, send1, own_ref):
    lane = iota((1, TL), 1)
    low = lane < 64
    sums = jnp.logical_and(lane % 64 >= 62, lane >= 0)
    blk[...] = jnp.zeros_like(blk)
    stage[...] = jnp.zeros_like(stage)
    jac32 = jac[...].astype(F32)
    for i in range(2):
        one = jac32[:, i, :]
        desc32 = desc_ref[i : i + 1, :].astype(F32)
        col = jnp.sum(one * desc32, axis=1, keepdims=True)
        high = col.astype(BF16).astype(F32)
        blk[i, 0, 0:NC, :] = one[:, 0:TL]
        blk[i, 0, NC : NC + 1, :] = desc32[:, 0:TL]
        blk[i, 1, 0:NC, 0 : ND - TL] = one[:, TL:ND]
        blk[i, 1, 0:NC, ND - TL : ND - TL + 1] = high
        blk[i, 1, 0:NC, ND - TL + 1 : ND - TL + 2] = col - high
        blk[i, 1, NC : NC + 1, 0 : ND - TL] = desc32[:, TL:ND]
        rest = blk[i, 1]
        both = rest + pltpu.roll(rest, 64, 1)
        is_desc = iota((PB, TL), 0) == NC
        rows = slice(PB * i, PB * i + PB)
        own_ref[rows, 0:TL] = blk[i, 0].astype(BF16)
        own_ref[rows, TL : 2 * TL] = jnp.where(sums, jnp.where(is_desc, -1.0, 0.0), both).astype(BF16)
        own_ref[rows, 2 * TL : 3 * TL] = rest.astype(BF16)
        even = blk[i, 1, pl.ds(0, NP, stride=2), :]
        odd = blk[i, 1, pl.ds(1, NP, stride=2), :]
        pair = jnp.where(low, even, pltpu.roll(odd, 64, 1))
        for q in range(NP):
            stage[q, 2 * i : 2 * i + 2, :] = blk[i, 0, 2 * q : 2 * q + 2, :]
            stage[q, 4 + i : 5 + i, :] = pair[q : q + 1, :]
    for q in range(NP):
        send1[q] = stage[q].astype(BF16)


def choices(order, panel, z, cap, step, one1, one2, flag, fast):
    base = panel[0] * TR
    lane = iota((8, TL), 1)
    sub = iota((8, TL), 0)
    parts = []
    line = jnp.zeros((8, TL), jnp.int32)
    for g in range(SLOTS // 8):
        part = jnp.zeros((8, TL), jnp.int32)
        for s in range(8 * g, 8 * g + 8):
            conf = order[base + s]
            part = jnp.where(sub == s - 8 * g, conf, part)
            line = jnp.where(lane == s, conf, line)
        parts.append(part)
    conf_col = jnp.concatenate(parts, axis=0)
    conf_row = jnp.concatenate([line] * 4, axis=0)
    plane_col = conf_col // (2 * NP)
    plane_row = conf_row // (2 * NP)
    slot_col = iota((SLOTS, TL), 0)
    slot_row = iota((SLOTS, TL), 1)
    same = plane_col == plane_row
    before = jnp.logical_and(same, slot_row < slot_col)
    rank_col = jnp.sum(jnp.where(before, 1.0, 0.0), axis=1, keepdims=True)
    if fast:
        flag[0] = jnp.where(jnp.max(rank_col) >= cap, 1, 0)
    rank_col = jnp.broadcast_to(rank_col, (SLOTS, TL)).astype(jnp.int32)
    place = rank_col if fast else slot_col
    here = plane_col == z
    device = (conf_col // 2) % NP
    which = conf_col % 2
    finds = []
    for kind in range(3):
        at = device * PR + (2 * which + kind if kind < 2 else 4 + which)
        find = []
        for t in range(NP * PR // TL):
            find.append(jnp.logical_and(at == slot_row + TL * t, here))
        finds.append(onehot(jnp.concatenate(find, axis=1)))
    goal = plane_col * step + place
    one2[...] = onehot(jnp.concatenate([goal == slot_row + TL * t for t in range(NZ * step // TL)], axis=1))
    finds = jnp.concatenate(finds, axis=0)
    if fast:
        after = jnp.logical_and(same, slot_col < slot_row)
        rank_row = jnp.sum(jnp.where(after, 1.0, 0.0), axis=0, keepdims=True).astype(jnp.int32)
        row = iota((one1.shape[0], SLOTS), 0)
        packs = []
        for kind in range(3):
            here_row = plane_row[0:1, 0:SLOTS] == z
            hit = jnp.logical_and(row == kind * step + rank_row[:, 0:SLOTS], rank_row[:, 0:SLOTS] < cap)
            packs.append(jnp.where(jnp.logical_and(hit, here_row), 1.0, 0.0))
        pack = jnp.concatenate(packs, axis=1).astype(BF16)
        one1[...] = dot(pack, finds, NN).astype(BF16)
    else:
        one1[...] = finds


def exchange(cap, step, total, fast, *refs):
    order_ref, panel_ref, jac_ref, desc_ref, inv_ref = refs[:5]
    if fast:
        own_ref, all_ref, inv_out, perm_out, over_ref = refs[5:10]
        rest = refs[10:]
    else:
        own_ref, all_ref = refs[5:7]
        inv_out = perm_out = over_ref = None
        rest = refs[7:]
    (flag, order, panel, jac, desc, inv, blk, stage, send1, got1, one1, send2, got2, one2, mine, ins,
     s1, r1, s2, r2, s4, r4, s5, r5, plane, line) = rest
    z = lax.axis_index("row")
    col = lax.axis_index("col")
    core = col % 2
    chip = col // 2
    sib = chip * 2 + 1 - core

    barrier = pltpu.get_barrier_semaphore()
    far = sorted(range(1, NZ), key=lambda d: -min(d, NZ - d))
    for d in far:
        pl.semaphore_signal(barrier, inc=1, device_id=((z + d) % NZ, 2 * chip + 1), device_id_type=MESH)
    for d in range(1, NCH):
        pl.semaphore_signal(barrier, inc=1, device_id=(z, (chip + d) % NCH * 2), device_id_type=MESH)

    @pl.when(core == 1)
    def _():
        pl.semaphore_signal(barrier, inc=1, device_id=(z, sib), device_id_type=MESH)

    loads = [(jac_ref, jac), (desc_ref, desc), (order_ref, order), (panel_ref, panel)]
    if fast:
        loads.append((inv_ref, inv))
    loads = [pltpu.make_async_copy(a, b, ins.at[n]) for n, (a, b) in enumerate(loads)]
    for load in loads:
        load.start()
    loads[0].wait()
    loads[1].wait()
    own_blocks(jac, desc, blk, stage, send1, own_ref)

    @pl.when(core == 0)
    def _():
        pl.semaphore_wait(barrier, NP - 1)
        pl.semaphore_signal(plane, inc=1, device_id=(z, sib), device_id_type=MESH)

    @pl.when(core == 1)
    def _():
        pl.semaphore_wait(plane, 1)

    x, y = chip // 4, chip % 4
    steps = [(dx, dy) for dx in range(4) for dy in range(4)]
    steps.sort(key=lambda d: min(d[0], 4 - d[0]) + min(d[1], 4 - d[1]), reverse=True)
    for dx, dy, dc in [(dx, dy, dc) for dx, dy in steps for dc in range(2)]:
        if not (dx or dy or dc):
            continue
        to = (((x + dx) % 4) * 4 + (y + dy) % 4) * 2 + (core + dc) % 2
        pltpu.make_async_remote_copy(
            send1.at[to], got1.at[col], s1, r1, device_id=(z, to), device_id_type=MESH
        ).start()
    got1[col] = send1[col]
    loads[2].wait()
    loads[3].wait()
    choices(order, panel, z, cap, step, one1, one2, flag, fast)
    if fast:
        told = pltpu.make_async_copy(flag, over_ref, ins.at[5])
        told.start()
        at = iota((PCOLS, PCOLS), 1)
        perm_out[...] = onehot(iota((PCOLS, PCOLS), 0) == (at % TR) * NC + at // TR)
        loads[4].wait()

    @pl.when(core == 1)
    def _():
        pl.semaphore_wait(barrier, 2 * (NZ - 1))
        pl.semaphore_signal(line, inc=1, device_id=(z, sib), device_id_type=MESH)

    @pl.when(core == 0)
    def _():
        pl.semaphore_wait(line, 1)

    pltpu.make_async_copy(got1.at[0 : NP - 1], got1.at[0 : NP - 1], r1).wait()

    held = got1[...].astype(F32).reshape(NP * PR, TL).astype(BF16)
    send2[...] = dot(one1[...], held, NN)[0:total, :].reshape(3, step // PR, PR, TL).astype(BF16)
    for d in far:
        for kind in range(3):
            pltpu.make_async_remote_copy(
                send2.at[kind], got2.at[kind, z], s2, r2.at[kind],
                device_id=((z + d) % NZ, col), device_id_type=MESH,
            ).start()
    for kind in range(3):
        got2[kind, z] = send2[kind]
    if fast:

        @pl.loop(0, 3)
        def _(g):
            rows = pl.ds(pl.multiple_of(g * 320, 320), 320)
            inv_out[rows, :] = dot(inv[rows, :], perm_out[...], NN).astype(BF16)

    steps = steps[:-1]
    for kind in range(3):
        part = got2.at[kind, 0 : NZ - 1]
        pltpu.make_async_copy(part, part, r2.at[kind]).wait()
        held = got2[kind].astype(F32).reshape(NZ * step, TL).astype(BF16)
        rows = pl.ds(kind * SLOTS, SLOTS)
        mine[rows, :] = dot(one2[...], held, NN).astype(BF16)
        for n, (dx, dy) in enumerate(steps):
            to = (((x + dx) % 4) * 4 + (y + dy) % 4) * 2 + core
            pltpu.make_async_remote_copy(
                mine.at[rows], all_ref.at[core, chip, rows], s4, r4.at[kind, n],
                device_id=(z, to), device_id_type=MESH,
            ).start()
        pltpu.make_async_remote_copy(
            mine.at[rows], all_ref.at[core, chip, rows], s5, r5, device_id=(z, sib), device_id_type=MESH
        ).start()
    all_ref[core, chip] = mine[...]
    for kind in range(3):
        rows = pl.ds(kind * SLOTS, SLOTS)
        for n, (dx, dy) in reversed(list(enumerate(steps))):
            source = ((x + 4 - dx) % 4) * 4 + (y + 4 - dy) % 4
            landed = all_ref.at[core, source, rows]
            pltpu.make_async_copy(landed, landed, r4.at[kind, n]).wait()
            pltpu.make_async_remote_copy(
                landed, landed, s5, r5, device_id=(z, sib), device_id_type=MESH
            ).start()
    other = all_ref.at[1 - core]
    pltpu.make_async_copy(other, other, r5).wait()

    pltpu.make_async_copy(got1.at[0 : NP - 1], got1.at[0 : NP - 1], s1).wait()
    every = got2.at[0:3, 0 : NZ - 1]
    pltpu.make_async_copy(every, every, s2).wait()
    pltpu.make_async_copy(all_ref.at[0, 0:15], all_ref.at[0, 0:15], s4).wait()
    pltpu.make_async_copy(other, other, s5).wait()
    if fast:
        told.wait()


def compute(own_ref, all_ref, inv_ref, perm_ref, factor_ref, next_ref, rhs, lhs, lhs2, dexp, cross, outs):
    width = 2.0 * math.sqrt(2.0 * ND)
    lane = iota((TR, TL), 1)
    low = lane < 64
    sums = lane % 64 >= 62
    last = jnp.logical_and(lane >= 62, low)

    def piece(row, kind, half):
        p = row // 2
        first = (kind * 2 + half) * TR
        return all_ref[p % 2, p // 2, first : first + TR, :]

    ds = []
    for half in range(2):
        for p in range(NC // 2 + 1):
            rest = piece(2 * p, 2, half).astype(F32)
            turned = pltpu.roll(rest, 64, 1)
            for odd in range(2):
                row = 2 * p + odd
                if row > NC:
                    continue
                xt = piece(row, odd, half)
                rows = slice(TR * row, TR * row + TR)
                mine = turned if odd else rest
                if row < NC:
                    rhs[half, rows, 0:TL] = xt
                    rhs[half, rows, TL : 2 * TL] = jnp.where(low != (odd == 1), rest, 0.0).astype(BF16)
                if half == 0:
                    both = jnp.where(low != (odd == 1), rest, turned)
                    lhs[rows, 0:TL] = xt
                    lhs[rows, TL : 2 * TL] = jnp.where(sums, -1.0 if row == NC else 0.0, both).astype(BF16)
                    if row < NC:
                        lhs2[rows, 0:TL] = xt
                        lhs2[rows, TL : 2 * TL] = mine.astype(BF16)
                if row == NC:
                    d0, d1 = xt.astype(F32), jnp.where(low, rest, 0.0)
                    ds.append((d0, d1))
                    e1 = jnp.where(last, -1.0, d1).astype(BF16)
                    for t in range(TL // TR):
                        to = slice(TL * half + TR * t, TL * half + TR * t + TR)
                        dexp[to, 0:TL] = xt
                        dexp[to, TL : 2 * TL] = e1

    zero = jnp.zeros((6, TL), F32)
    own_d = [own_ref[PB * i + NC - 12 : PB * i + PB - 0, :].astype(F32)[12:13] for i in range(2)]
    d0s = jnp.concatenate([ds[0][0]] + [d[:, 0:TL] for d in own_d] + [zero], axis=0)
    d1s = jnp.concatenate([ds[0][1]] + [jnp.where(low[0:1], d[:, 2 * TL :], 0.0) for d in own_d] + [zero], axis=0)
    f1s, f2s = [], []
    lane24 = iota((24, TL), 1) % TR
    for half in range(2):
        dist = jnp.zeros((24, TL), F32)
        for b in range(TR):
            u0 = d0s - ds[half][0][b : b + 1, :]
            u1 = d1s - ds[half][1][b : b + 1, :]
            dist = jnp.where(lane24 == b, jnp.sum(u0 * u0 + u1 * u1, axis=1, keepdims=True), dist)
        scaled = (math.sqrt(5.0) / width) * jnp.sqrt(dist)
        decay = jnp.exp(-scaled)
        f1s.append(decay * (1.0 + scaled))
        f2s.append(decay * (5.0 / (width * width)))

    def wide(tile):
        return jnp.concatenate([tile] * 8, axis=1)[:, 0:PCOLS]

    own_lhs = own_ref[:, 0 : 2 * TL]
    own_lhs2 = jnp.concatenate([own_ref[:, 0:TL], own_ref[:, 2 * TL :]], axis=1)
    prod2 = dot(own_lhs2, dexp[...], NT)
    tiles = []
    for half in range(2):
        prod = dot(own_lhs, rhs[half], NT)
        parts = []
        for i in range(2):
            rows = slice(PB * i, PB * i + PB)
            f1 = wide(f1s[half][TR + i : TR + i + 1, :])
            qq = wide(f2s[half][TR + i : TR + i + 1, :]) * prod[PB * i + NC : PB * i + NC + 1, :]
            p = wide(prod2[rows, TL * half : TL * half + TL])
            parts.append(prod[rows, :] * f1 + p * qq)
        tiles.append(jnp.concatenate(parts, axis=0))
    factor = dot(tiles[0].astype(BF16), inv_ref[...], NT)
    outs[0:NC, :] = factor[0:NC, :]
    outs[NC : 2 * NC, :] = factor[PB : PB + NC, :]
    factor_ref[...] = outs[...].astype(BF16)
    most = jnp.max(jnp.abs(factor), axis=1, keepdims=True)
    scale = jnp.ones_like(most)
    back = jnp.ones_like(most)
    for _ in range(4):
        large = most * scale > 2.0**24
        scale = jnp.where(large, scale * 2.0**-24, scale)
        back = jnp.where(large, back * 2.0**24, back)
    scaled_factor = (factor.astype(BF16).astype(F32) * scale).astype(BF16)

    qq = wide(f2s[1][0:TR, :]) * dot(lhs[PCOLS : PCOLS + TR, :], rhs[1], NT)
    f1 = wide(f1s[1][0:TR, :])

    for g in range(4):
        rows = slice(240 * g, 240 * g + 240)
        a = dot(lhs[rows, :], rhs[1], NT)
        b = dot(lhs2[rows, :], dexp[TL : 2 * TL, :], NT)
        got = []
        for n in range(15):
            part = slice(TR * n, TR * n + TR)
            got.append((a[part, :] * f1 + wide(b[part, :]) * qq).astype(BF16))
        cross[rows, :] = jnp.concatenate(got, axis=0)

    middle = dot(scaled_factor, inv_ref[...], NN)
    high = middle.astype(BF16)
    both = jnp.concatenate([high, (middle - high.astype(F32)).astype(BF16)], axis=0)
    change = dot(both, cross[...], NN)
    change = (change[0:TL, :] + change[TL : 2 * TL, :]) * back
    updated = (tiles[1] - change).astype(BF16)
    final = dot(updated, perm_ref[...], NT)
    outs[0:NC, :] = final[0:NC, :]
    outs[NC : 2 * NC, :] = final[PB : PB + NC, :]
    next_ref[...] = outs[...].astype(BF16)


VM = pl.BlockSpec(memory_space=pltpu.VMEM)
HBM = pl.BlockSpec(memory_space=pltpu.HBM)


def run_exchange(fast, order, panel, jac, desc, inv):
    cap, step, total = (8, 8, 24) if fast else (32, 32, 96)
    square = jax.ShapeDtypeStruct((PCOLS, PCOLS), BF16)
    outs = (
        jax.ShapeDtypeStruct((2 * PB, 3 * TL), BF16),
        jax.ShapeDtypeStruct((2, NCH, 3 * SLOTS, TL), BF16),
    )
    specs = (VM, VM)
    if fast:
        outs += (square, square, jax.ShapeDtypeStruct((1,), jnp.int32))
        specs += (VM, VM, HBM)
    dma = pltpu.SemaphoreType.DMA
    return pl.pallas_call(
        functools.partial(exchange, cap, step, total, fast),
        name="exchange" if fast else "exchange_full",
        out_shape=outs,
        in_specs=[HBM] * 5,
        out_specs=specs,
        scratch_shapes=[
            pltpu.SMEM((1,), jnp.int32),
            pltpu.SMEM((NZ * 2 * NP,), jnp.int32),
            pltpu.SMEM((1,), jnp.int32),
            pltpu.VMEM(jac.shape, BF16),
            pltpu.VMEM(desc.shape, BF16),
            pltpu.VMEM((PCOLS, PCOLS) if fast else (TR, TL), BF16),
            pltpu.VMEM((2, 2, PB, TL), F32),
            pltpu.VMEM((NP, PR, TL), F32),
            pltpu.VMEM((NP, PR, TL), BF16),
            pltpu.VMEM((NP, PR, TL), BF16),
            pltpu.VMEM((-(-total // TR) * TR, NP * PR), BF16),
            pltpu.VMEM((3, step // PR, PR, TL), BF16),
            pltpu.VMEM((3, NZ, step // PR, PR, TL), BF16),
            pltpu.VMEM((SLOTS, NZ * step), BF16),
            pltpu.VMEM((3 * SLOTS, TL), BF16),
            dma((6,)), dma, dma, dma, dma((3,)), dma, dma((3, NCH - 1)), dma, dma,
            pltpu.SemaphoreType.REGULAR, pltpu.SemaphoreType.REGULAR,
        ],
        compiler_params=pltpu.CompilerParams(
            collective_id=0 if fast else 1, has_side_effects=True, vmem_limit_bytes=24 * 2**20
        ),
    )(order, panel, jac, desc, inv)


def run_compute(own, everything, inv, perm):
    rows = 2 * NC
    return pl.pallas_call(
        compute,
        name="compute",
        out_shape=(jax.ShapeDtypeStruct((rows, PCOLS), BF16),) * 2,
        in_specs=[VM] * 4,
        out_specs=(VM, VM),
        scratch_shapes=[
            pltpu.VMEM((2, PCOLS, 2 * TL), BF16),
            pltpu.VMEM((PCOLS + TR, 2 * TL), BF16),
            pltpu.VMEM((PCOLS, 2 * TL), BF16),
            pltpu.VMEM((2 * TL, 2 * TL), BF16),
            pltpu.VMEM((PCOLS, PCOLS), BF16),
            pltpu.VMEM((rows, PCOLS), F32),
        ],
        compiler_params=pltpu.CompilerParams(vmem_limit_bytes=40 * 2**20),
    )(own, everything, inv, perm)


def shards(jacobians, descriptors, block_inverse, tile_order, panel):
    jac = jnp.transpose(jacobians, (1, 0, 2))
    args = (tile_order, panel, jac, descriptors, block_inverse)
    own, few, inv, perm, over = run_exchange(True, *args)

    outs = run_compute(own, few, inv, perm)

    def usual(outs):
        return outs

    def crowded(outs):
        again, everything = run_exchange(False, *args)
        return run_compute(again, everything, inv, perm)

    return lax.cond(over[0] == 0, usual, crowded, outs)


def solution(mesh):
    placed = (P(("row", "col"), None, None), P(("row", "col"), None), P(), P(), P())
    return jax.shard_map(
        shards,
        mesh=mesh,
        in_specs=placed,
        out_specs=(P(("row", "col"), None), P(("row", "col"), None)),
        check_vma=False,
    )
```
